128 devices in a mesh: gx: 16 (over z, y_hi, core), gy: 8 (over x, y_lo).
Axes of the slice: x: 4, y: 4 (y_hi: 2, y_lo: 2; y = y_hi * 2 + y_lo), z: 4, core: 2. Of those that a mesh axis runs over, the one named last changes fastest.
Arguments:
- state: float32 [4, 256, 128, 128], P(None, 'gx', 'gy'), may hold values from -4 to 4
- offsets: int32 [2], replicated, may hold values from 0 to 127
Outputs:
- advanced: float32 [4, 256, 128, 128], P(None, 'gx', 'gy')
The draws below stay inside these ranges and needn't reach their ends.
All inputs are finite; a program needn't handle non-finite values.
Results may differ from the reference program's by a relative error of at most 0.00002.
Values sent between devices are 32-bit elements; how exact they have to be, the bound alone decides.
A program may use at most 64 MiB of HBM per device.

```python
import jax
import jax.numpy as jnp

NZ = 128
RELAX = 4
STEPS = 2
NX = 256
NY = 128


def steps_of(stream_key, dims, cuts, least, top_value):
    factor_of, own = 1.0, jax.random.fold_in(stream_key, 6)
    for dim, blocks in cuts:
        draws = jnp.exp(jax.random.uniform(jax.random.fold_in(own, dim), (blocks,), jnp.float32, least / len(cuts), top_value / len(cuts)))
        factor_of = factor_of * jnp.repeat(draws, dims[dim] // blocks).reshape([-1 if axis == dim else 1 for axis in range(len(dims))])
    return factor_of


def noise(own_key, shape, scale, limit, pieces=(), held_as=jnp.bfloat16):
    entries = scale * jax.random.normal(own_key, shape, jnp.float32)
    if pieces:
        entries = entries * steps_of(own_key, shape, pieces, -0.22, 0.18)
    return jnp.clip(entries, -limit, limit).astype(held_as)


def setup_inputs(seed: int = 0) -> dict:
    seeds = jax.random.split(jax.random.key(seed), 3)
    return {
        "state": noise(seeds[0], (4, NX, NY, NZ), 0.5, 4.0, ((1, 16), (2, 8)), jnp.float32),
        "offsets": jax.random.randint(seeds[1], (STEPS,), 0, NY).astype(jnp.int32),
    }


time_step = 0.2
viscosity = 0.1


def extend(field, offset, width):
    left = jnp.roll(field[:, -width:], offset, axis=2)
    right = jnp.roll(field[:, :width], -offset, axis=2)
    grown = jnp.concatenate([left, field, right], axis=1)
    return jnp.concatenate([grown[:, :, -width:], grown, grown[:, :, :width]], axis=2)


def shrink(ext):
    return ext[..., 1:-1, 1:-1, :]


def diff_x(ext):
    return (ext[..., 2:, 1:-1, :] - ext[..., :-2, 1:-1, :]) * 0.5


def diff_y(ext):
    return (ext[..., 1:-1, 2:, :] - ext[..., 1:-1, :-2, :]) * 0.5


def diff_z(center):
    return (jnp.roll(center, -1, -1) - jnp.roll(center, 1, -1)) * 0.5


def beside_all(ext):
    center = shrink(ext)
    total = ext[..., 2:, 1:-1, :] + ext[..., :-2, 1:-1, :]
    total = total + ext[..., 1:-1, 2:, :] + ext[..., 1:-1, :-2, :]
    return total + jnp.roll(center, -1, -1) + jnp.roll(center, 1, -1)


def advance(state, offset):
    shear = 2.0 / NX
    xpos = jnp.arange(NX).astype(jnp.float32)
    mean_flow = (shear * (xpos + 0.5 - NX / 2.0))[:, None, None]
    ext = extend(state, offset, 1)
    speed_x, speed_y, speed_z = state[0], state[1], state[2]
    carried = speed_x * diff_x(ext) + (speed_y + mean_flow) * diff_y(ext) + speed_z * diff_z(state)
    tendency = viscosity * (beside_all(ext) - 6.0 * state) - carried
    zeros = jnp.zeros_like(speed_x)
    source = jnp.stack([zeros, -shear * speed_x, zeros, -speed_x])
    provisional = state + time_step * (tendency + source)
    velo = extend(provisional[:3], offset, 1)
    rhs = (diff_x(velo[0]) + diff_y(velo[1]) + diff_z(provisional[2])) / time_step
    pressure = -rhs / 6.0
    for sweep in range(RELAX):
        padded = extend(pressure[None], offset, 1)[0]
        pressure = (beside_all(padded) - rhs) / 6.0
    padded = extend(pressure[None], offset, 1)[0]
    new_x = provisional[0] - time_step * diff_x(padded)
    new_y = provisional[1] - time_step * diff_y(padded)
    new_z = provisional[2] - time_step * diff_z(pressure)
    return jnp.stack([new_x, new_y, new_z, provisional[3]])


def reference(state, offsets):
    for step in range(STEPS):
        state = advance(state, offsets[step])
    return state
```

```python
import functools

import jax
import jax.numpy as jnp
from jax import lax
from jax.experimental import pallas as pl
from jax.experimental.pallas import tpu as pltpu
from jax.sharding import PartitionSpec as P

RELAX = 4
DEEP = RELAX + 1

time_step = 0.2
viscosity = 0.1

MESH = pl.DeviceIdType.MESH
ROW = 8
TALL = 32


def across(x, shift):
    return pltpu.roll(x, shift % x.shape[-1], x.ndim - 1)


def stencil(c, xm, xp, ym, yp):
    zp, zm = across(c, -1), across(c, 1)
    total = (xp + xm) + (yp + ym) + (zp + zm)
    return total, xp - xm, yp - ym, zp - zm


def kernel(ngx, ngy, steps, offsets, state, out, ext, prov, rhs, press, final,
           x_send, x_recv, y_send, y_recv, c_send, c_recv, send_sem, recv_sem, shear_out, shear_in, local_sem, *shear_recv):
    slab, rows = state.shape[1], state.shape[2]
    gx, gy = lax.axis_index("gx"), lax.axis_index("gy")
    below, above = lax.rem(gx + ngx - 1, ngx), lax.rem(gx + 1, ngx)
    left, right = lax.rem(gy + ngy - 1, ngy), lax.rem(gy + 1, ngy)
    at_x = {-1: below, 0: gx, 1: above}
    at_y = {-1: left, 0: gy, 1: right}
    has = {-1: gx > 0, 1: gx < ngx - 1}
    ends = {-1: gx == 0, 1: gx == ngx - 1}
    far = {-1: ngx - 1, 1: 0}
    total_x = slab * ngx
    rate = 2.0 / total_x
    own = pl.ds(ROW, rows)

    fetch = pltpu.make_async_copy(state, ext.at[0, :, pl.ds(2, slab), own, :], local_sem.at[0])
    fetch.start()

    barrier = pltpu.get_barrier_semaphore()

    def greet(x, y):
        pl.semaphore_signal(barrier, inc=1, device_id=(x, y), device_id_type=MESH)

    for dy in (-1, 1):
        greet(gx, at_y[dy])
    for dx in (-1, 1):
        @pl.when(has[dx])
        def _():
            for dy in (-1, 0, 1):
                greet(at_x[dx], at_y[dy])

        @pl.when(ends[dx])
        def _():
            for k in range(ngy):
                greet(far[dx], k)

    def remote(src, dst, send, recv, x, y):
        return pltpu.make_async_remote_copy(
            src_ref=src, dst_ref=dst, send_sem=send, recv_sem=recv,
            device_id=(x, y), device_id_type=MESH)

    def rim(side, width, size):
        return (0, size) if side < 0 else (size - width, -width)

    def messages(step, part, dx, dy):
        dev = at_x[dx], at_y[dy]
        if dx == 0:
            n = m = (dy + 1) // 2
            src, dst = y_send.at[step, part, m], y_recv.at[step, part, m]
        elif dy == 0:
            m = (dx + 1) // 2
            n = 2 + m
            src, dst = x_send.at[step, part, m], x_recv.at[step, part, m]
        else:
            m = (dx + 1) + (dy + 1) // 2
            n = 4 + m
            size = pl.ds(0, 8 if part == 0 else 16)
            src, dst = c_send.at[step, part, m, size, :], c_recv.at[step, part, m, size, :]
        return remote(src, dst, send_sem.at[step, part, n], recv_sem.at[step, part, n], *dev)

    def shear_slot(step, part, k):
        return shear_recv[2 * step + part].at[:, pl.ds(k * (rows // 8), rows // 8), :, :]

    def shear_message(step, part, dx, k):
        return remote(x_send.at[step, part, (dx + 1) // 2], shear_slot(step, part, gy),
                      shear_out.at[step, part, k], shear_in.at[step, part, gy], far[dx], k)

    def shear_arrival(step, part, dx, k):
        slot = shear_slot(step, part, k)
        return remote(slot, slot, shear_out.at[step, part, k], shear_in.at[step, part, k], far[dx], k)

    def field_planes(dx, ghost):
        s2, d2 = rim(dx, 2, slab)
        s1, d1 = rim(dx, 1, slab)
        p2, p1 = (d2, d1) if ghost else (s2, s1)
        return [(0, 2 + p2), (0, 3 + p2), (1, 2 + p1), (2, 2 + p1), (3, 2 + p1)]

    def lines(part, dy, ghost):
        if part == 0:
            s2, d2 = rim(dy, 2, rows)
            s1, d1 = rim(dy, 1, rows)
            p2, p1 = (d2, d1) if ghost else (s2, s1)
            return [(f * (slab + 4) + 2) * TALL + ROW + y
                    for f, y in ((1, p2), (1, p2 + 1), (0, p1), (2, p1), (3, p1))]
        s, d = rim(dy, DEEP, rows)
        return [DEEP * TALL + ROW + (d if ghost else s) + k for k in range(DEEP)]

    def flattened(step, part):
        if part == 0:
            return ext.at[step].reshape(4 * (slab + 4) * TALL, 128)
        return rhs.at[step].reshape((slab + 2 * DEEP) * TALL, 128)

    def pack(step, part):
        for dx in (-1, 1):
            m = (dx + 1) // 2
            for n in range(DEEP):
                if part == 0:
                    f, X = field_planes(dx, False)[n]
                else:
                    X = DEEP + rim(dx, DEEP, slab)[0] + n
                for c in range(rows // 8):
                    piece = slice(ROW + 8 * c, ROW + 8 * c + 8)
                    x_send[step, part, m, n, c] = ext[step, f, X, piece] if part == 0 else rhs[step, X, piece]
        flat = flattened(step, part)
        for dy in (-1, 1):
            for n, base in enumerate(lines(part, dy, False)):
                y_send[step, part, (dy + 1) // 2, n] = flat[pl.ds(base, slab, stride=TALL), :]
        w = 1 if part == 0 else DEEP - 1
        for dx in (-1, 1):
            for dy in (-1, 1):
                m = (dx + 1) + (dy + 1) // 2
                x, y = rim(dx, w, slab)[0], ROW + rim(dy, w, rows)[0]
                if part == 0:
                    for f in range(2):
                        c_send[step, part, m, f:f + 1] = ext[step, f, 2 + x, y:y + 1]
                else:
                    for n in range(w):
                        c_send[step, part, m, w * n:w * n + w] = rhs[step, DEEP + x + n, y:y + w]

    def start_all(step, part):
        for dx in (-1, 1):
            @pl.when(ends[dx])
            def _():
                for k in range(ngy):
                    shear_message(step, part, dx, k).start()
        for dx in (-1, 1):
            @pl.when(has[dx])
            def _():
                for dy in (0, -1, 1):
                    messages(step, part, dx, dy).start()
        for dy in (-1, 1):
            messages(step, part, 0, dy).start()

    def sheared(step, part, dx):
        span = rows * ngy
        shift = span - offsets[step] if dx > 0 else offsets[step]
        start = lax.rem(gy * rows + shift + (span - ROW), span)
        block, within = lax.div(start, 8), lax.rem(start, 8)
        blocks = [lax.rem(block + c, span // 8) for c in range(TALL // 8 + 1)]
        for n in range(DEEP):
            tall = jnp.concatenate([shear_recv[2 * step + part][n, at] for at in blocks], axis=0)
            plane = pltpu.roll(tall, TALL + 8 - within, 0)[:TALL]
            if part == 0:
                f, X = field_planes(dx, True)[n]
                ext[step, f, X] = plane
            else:
                rhs[step, DEEP + rim(dx, DEEP, slab)[1] + n] = plane

    def unpack_x(step, part, dx):
        m = (dx + 1) // 2
        for n in range(DEEP):
            if part == 0:
                f, X = field_planes(dx, True)[n]
            else:
                X = DEEP + rim(dx, DEEP, slab)[1] + n
            for c in range(rows // 8):
                piece = slice(ROW + 8 * c, ROW + 8 * c + 8)
                value = x_recv[step, part, m, n, c]
                if part == 0:
                    ext[step, f, X, piece] = value
                else:
                    rhs[step, X, piece] = value

    def unpack_corner(step, part, dx, dy):
        m = (dx + 1) + (dy + 1) // 2
        w = 1 if part == 0 else DEEP - 1
        x, y = rim(dx, w, slab)[1], ROW + rim(dy, w, rows)[1]
        if part == 0:
            for f in range(2):
                ext[step, f, 2 + x, y:y + 1] = c_recv[step, part, m, f:f + 1]
        else:
            for n in range(w):
                rhs[step, DEEP + x + n, y:y + w] = c_recv[step, part, m, w * n:w * n + w]

    def arrive_all(step, part):
        flat = flattened(step, part)
        for dy in (-1, 1):
            messages(step, part, 0, dy).wait_recv()
            for n, base in enumerate(lines(part, dy, True)):
                flat[pl.ds(base, slab, stride=TALL), :] = y_recv[step, part, (dy + 1) // 2, n]
        for dx in (-1, 1):
            @pl.when(has[-dx])
            def _():
                messages(step, part, dx, 0).wait_recv()
                unpack_x(step, part, dx)
                for dy in (-1, 1):
                    messages(step, part, dx, dy).wait_recv()
                    unpack_corner(step, part, dx, dy)
        for dx in (-1, 1):
            @pl.when(ends[-dx])
            def _():
                for k in range(ngy):
                    shear_arrival(step, part, -dx, k).wait_recv()
                sheared(step, part, dx)

    def sent_all(step, part):
        for dy in (-1, 1):
            messages(step, part, 0, dy).wait_send()
        for dx in (-1, 1):
            @pl.when(has[dx])
            def _():
                for dy in (0, -1, 1):
                    messages(step, part, dx, dy).wait_send()

            @pl.when(ends[dx])
            def _():
                for k in range(ngy):
                    shear_message(step, part, dx, k).wait_send()

    half = -0.5 * time_step
    keep = 1.0 - 6.0 * time_step * viscosity
    spread = time_step * viscosity

    def move(c, parts, hu, hv, hw):
        total, ddx, ddy, ddz = parts
        return (keep * c + spread * total) + (hu * ddx + hv * ddy + hw * ddz)

    def mean_flow(x):
        return rate * (x.astype(jnp.float32) + (0.5 - total_x / 2.0))

    lo, hi = ROW, ROW + rows

    def provisional(step):
        e = ext.at[step]

        def around(f, X):
            c = e[f, X, lo:hi]
            return c, stencil(c, e[f, X - 1, lo:hi], e[f, X + 1, lo:hi],
                              e[f, X, lo - 1:hi - 1], e[f, X, lo + 1:hi + 1])

        def speeds(X):
            flow = mean_flow(lax.rem(gx * slab + (X - 2) + total_x, total_x))
            u, v, w = e[0, X, lo:hi], e[1, X, lo:hi], e[2, X, lo:hi]
            return u, half * u, half * (v + flow), half * w

        def plane(i, _):
            X = i + 2
            u, hu, hv, hw = speeds(X)
            for f in range(4):
                c, parts = around(f, X)
                value = move(c, parts, hu, hv, hw)
                if f == 1:
                    value = value - (time_step * rate) * u
                if f == 3:
                    value = value - time_step * u
                prov[f, i + 1, lo:hi] = value
            return 0

        lax.fori_loop(0, slab, plane, 0)
        for X in (1, slab + 2):
            u, hu, hv, hw = speeds(X)
            c, parts = around(0, X)
            prov[0, X - 1, lo:hi] = move(c, parts, hu, hv, hw)
        flat = e.reshape(4 * (slab + 4) * TALL, 128)
        into = prov.reshape(4 * (slab + 2) * TALL, 128)
        place = gx * slab + lax.broadcasted_iota(jnp.int32, (slab, 128), 0)
        flow = mean_flow(place)
        for y in (-1, rows):
            def line(f, x, yy):
                return flat[pl.ds((f * (slab + 4) + 2 + x) * TALL + ROW + yy, slab, stride=TALL), :]

            u, c, w = line(0, 0, y), line(1, 0, y), line(2, 0, y)
            parts = stencil(c, line(1, -1, y), line(1, 1, y), line(1, 0, y - 1), line(1, 0, y + 1))
            value = move(c, parts, half * u, half * (c + flow), half * w) - (time_step * rate) * u
            into[pl.ds((slab + 2 + 1) * TALL + ROW + y, slab, stride=TALL), :] = value

    def divergence(step):
        scale = 0.5 / (6.0 * time_step)

        def plane(i, _):
            dx = prov[0, i + 2, lo:hi] - prov[0, i, lo:hi]
            dy = prov[1, i + 1, lo + 1:hi + 1] - prov[1, i + 1, lo - 1:hi - 1]
            w = prov[2, i + 1, lo:hi]
            rhs[step, DEEP + i, lo:hi] = scale * (dx + dy + (across(w, -1) - across(w, 1)))
            return 0

        lax.fori_loop(0, slab, plane, 0)

    def relax(step):
        r = rhs.at[step]
        top, bottom = ROW - RELAX, ROW + rows + RELAX

        def first(X, _):
            c = r[X, top:bottom]
            total = stencil(c, r[X - 1, top:bottom], r[X + 1, top:bottom],
                            r[X, top - 1:bottom - 1], r[X, top + 1:bottom + 1])[0]
            press[0, X, top:bottom] = -(total * (1.0 / 6.0) + c)
            return 0

        lax.fori_loop(1, slab + 2 * DEEP - 1, first, 0)
        for k in range(1, RELAX):
            old, new = press.at[k - 1], press.at[k]

            def sweep(X, _):
                c = old[X, top:bottom]
                total = stencil(c, old[X - 1, top:bottom], old[X + 1, top:bottom],
                                old[X, top - 1:bottom - 1], old[X, top + 1:bottom + 1])[0]
                new[X, top:bottom] = total * (1.0 / 6.0) - r[X, top:bottom]
                return 0

            lax.fori_loop(1 + k, slab + 2 * DEEP - 1 - k, sweep, 0)

    def project(step, store):
        p = press.at[RELAX - 1]

        def plane(i, _):
            X = DEEP + i
            c = p[X, lo:hi]
            store(0, i, prov[0, i + 1, lo:hi] + half * (p[X + 1, lo:hi] - p[X - 1, lo:hi]))
            store(1, i, prov[1, i + 1, lo:hi] + half * (p[X, lo + 1:hi + 1] - p[X, lo - 1:hi - 1]))
            store(2, i, prov[2, i + 1, lo:hi] + half * (across(c, -1) - across(c, 1)))
            store(3, i, prov[3, i + 1, lo:hi])
            return 0

        lax.fori_loop(0, slab, plane, 0)

    fetch.wait()
    for step in range(steps):
        pack(step, 0)
        if step == 0:
            inner = jnp.logical_and(gx > 0, gx < ngx - 1)

            @pl.when(inner)
            def _():
                pl.semaphore_wait(barrier, 8)

            @pl.when(jnp.logical_not(inner))
            def _():
                pl.semaphore_wait(barrier, 5 + ngy)

        start_all(step, 0)
        arrive_all(step, 0)
        provisional(step)
        divergence(step)
        pack(step, 1)
        start_all(step, 1)
        arrive_all(step, 1)
        relax(step)
        if step < steps - 1:
            def store(f, i, value, step=step):
                ext[step + 1, f, i + 2, lo:hi] = value
        else:
            def store(f, i, value):
                final[f, i] = value
        project(step, store)

    give = pltpu.make_async_copy(final, out, local_sem.at[1])
    give.start()
    for step in range(steps):
        for part in range(2):
            sent_all(step, part)
    give.wait()


def local(ngx, ngy, state, offsets):
    steps = offsets.shape[0]
    fields, slab, rows, depth = state.shape
    f32 = jnp.float32
    return pl.pallas_call(
        functools.partial(kernel, ngx, ngy, steps),
        out_shape=jax.ShapeDtypeStruct(state.shape, f32),
        in_specs=[pl.BlockSpec(memory_space=pltpu.SMEM), pl.BlockSpec(memory_space=pl.ANY)],
        out_specs=pl.BlockSpec(memory_space=pl.ANY),
        scratch_shapes=[
            pltpu.VMEM((steps, fields, slab + 4, TALL, depth), f32),
            pltpu.VMEM((fields, slab + 2, TALL, depth), f32),
            pltpu.VMEM((steps, slab + 2 * DEEP, TALL, depth), f32),
            pltpu.VMEM((RELAX, slab + 2 * DEEP, TALL, depth), f32),
            pltpu.VMEM(state.shape, f32),
            pltpu.VMEM((steps, 2, 2, DEEP, rows // 8, 8, depth), f32),
            pltpu.VMEM((steps, 2, 2, DEEP, rows // 8, 8, depth), f32),
            pltpu.VMEM((steps, 2, 2, DEEP, slab, depth), f32),
            pltpu.VMEM((steps, 2, 2, DEEP, slab, depth), f32),
            pltpu.VMEM((steps, 2, 4, 16, depth), f32),
            pltpu.VMEM((steps, 2, 4, 16, depth), f32),
            pltpu.SemaphoreType.DMA((steps, 2, 8)),
            pltpu.SemaphoreType.DMA((steps, 2, 8)),
            pltpu.SemaphoreType.DMA((steps, 2, ngy)),
            pltpu.SemaphoreType.DMA((steps, 2, ngy)),
            pltpu.SemaphoreType.DMA((2,)),
        ] + [pltpu.VMEM((DEEP, ngy * rows // 8, 8, depth), f32)] * (2 * steps),
        compiler_params=pltpu.CompilerParams(
            collective_id=0, has_side_effects=True, vmem_limit_bytes=32 * 1024 * 1024
        ),
    )(offsets, state)


def solution(mesh):
    in_specs = (P(None, "gx", "gy", None), P())
    out_specs = P(None, "gx", "gy", None)
    body = functools.partial(local, mesh.shape["gx"], mesh.shape["gy"])
    return jax.shard_map(body, mesh=mesh, in_specs=in_specs, out_specs=out_specs, check_vma=False)
```

```python
import functools

import jax
import jax.numpy as jnp
from jax import lax
from jax.experimental import pallas as pl
from jax.experimental.pallas import tpu as pltpu
from jax.sharding import PartitionSpec as P

RELAX = 4
DEEP = RELAX + 1

time_step = 0.2
viscosity = 0.1

MESH = pl.DeviceIdType.MESH
ROW = 8
TALL = 32


def across(x, shift):
    return pltpu.roll(x, shift % x.shape[-1], x.ndim - 1)


def stencil(c, xm, xp, ym, yp):
    zp, zm = across(c, -1), across(c, 1)
    total = (xp + xm) + (yp + ym) + (zp + zm)
    return total, xp - xm, yp - ym, zp - zm


def loop(first, last, body):
    for n in range(first, last):
        body(n, 0)


def kernel(ngx, ngy, steps, offsets, state, out, ext, prov, rhs, press, final,
           x_send, x_recv, y_send, y_recv, c_send, c_recv, send_sem, recv_sem, shear_out, shear_in, local_sem, *shear_recv):
    slab, rows = state.shape[1], state.shape[2]
    gx, gy = lax.axis_index("gx"), lax.axis_index("gy")
    below, above = lax.rem(gx + ngx - 1, ngx), lax.rem(gx + 1, ngx)
    left, right = lax.rem(gy + ngy - 1, ngy), lax.rem(gy + 1, ngy)
    at_x = {-1: below, 0: gx, 1: above}
    at_y = {-1: left, 0: gy, 1: right}
    has = {-1: gx > 0, 1: gx < ngx - 1}
    ends = {-1: gx == 0, 1: gx == ngx - 1}
    far = {-1: ngx - 1, 1: 0}
    total_x = slab * ngx
    rate = 2.0 / total_x
    own = pl.ds(ROW, rows)

    fetch = pltpu.make_async_copy(state, ext.at[0, :, pl.ds(2, slab), own, :], local_sem.at[0])
    fetch.start()

    barrier = pltpu.get_barrier_semaphore()

    def greet(x, y):
        pl.semaphore_signal(barrier, inc=1, device_id=(x, y), device_id_type=MESH)

    for dy in (-1, 1):
        greet(gx, at_y[dy])
    for dx in (-1, 1):
        @pl.when(has[dx])
        def _():
            for dy in (-1, 0, 1):
                greet(at_x[dx], at_y[dy])

        @pl.when(ends[dx])
        def _():
            for k in range(ngy):
                greet(far[dx], k)

    def remote(src, dst, send, recv, x, y):
        return pltpu.make_async_remote_copy(
            src_ref=src, dst_ref=dst, send_sem=send, recv_sem=recv,
            device_id=(x, y), device_id_type=MESH)

    def rim(side, width, size):
        return (0, size) if side < 0 else (size - width, -width)

    def messages(step, part, dx, dy):
        dev = at_x[dx], at_y[dy]
        if dx == 0:
            n = m = (dy + 1) // 2
            src, dst = y_send.at[step, part, m], y_recv.at[step, part, m]
        elif dy == 0:
            m = (dx + 1) // 2
            n = 2 + m
            src, dst = x_send.at[step, part, m], x_recv.at[step, part, m]
        else:
            m = (dx + 1) + (dy + 1) // 2
            n = 4 + m
            size = pl.ds(0, 8 if part == 0 else 16)
            src, dst = c_send.at[step, part, m, size, :], c_recv.at[step, part, m, size, :]
        return remote(src, dst, send_sem.at[step, part, n], recv_sem.at[step, part, n], *dev)

    def shear_slot(step, part, k):
        return shear_recv[2 * step + part].at[:, pl.ds(k * (rows // 8), rows // 8), :, :]

    def shear_message(step, part, dx, k):
        return remote(x_send.at[step, part, (dx + 1) // 2], shear_slot(step, part, gy),
                      shear_out.at[step, part, k], shear_in.at[step, part, gy], far[dx], k)

    def shear_arrival(step, part, dx, k):
        slot = shear_slot(step, part, k)
        return remote(slot, slot, shear_out.at[step, part, k], shear_in.at[step, part, k], far[dx], k)

    def field_planes(dx, ghost):
        s2, d2 = rim(dx, 2, slab)
        s1, d1 = rim(dx, 1, slab)
        p2, p1 = (d2, d1) if ghost else (s2, s1)
        return [(0, 2 + p2), (0, 3 + p2), (1, 2 + p1), (2, 2 + p1), (3, 2 + p1)]

    def lines(part, dy, ghost):
        if part == 0:
            s2, d2 = rim(dy, 2, rows)
            s1, d1 = rim(dy, 1, rows)
            p2, p1 = (d2, d1) if ghost else (s2, s1)
            return [(f * (slab + 4) + 2) * TALL + ROW + y
                    for f, y in ((1, p2), (1, p2 + 1), (0, p1), (2, p1), (3, p1))]
        s, d = rim(dy, DEEP, rows)
        return [DEEP * TALL + ROW + (d if ghost else s) + k for k in range(DEEP)]

    def flattened(step, part):
        if part == 0:
            return ext.at[step].reshape(4 * (slab + 4) * TALL, 128)
        return rhs.at[step].reshape((slab + 2 * DEEP) * TALL, 128)

    def pack(step, part):
        for dx in (-1, 1):
            m = (dx + 1) // 2
            for n in range(DEEP):
                if part == 0:
                    f, X = field_planes(dx, False)[n]
                else:
                    X = DEEP + rim(dx, DEEP, slab)[0] + n
                for c in range(rows // 8):
                    piece = slice(ROW + 8 * c, ROW + 8 * c + 8)
                    x_send[step, part, m, n, c] = ext[step, f, X, piece] if part == 0 else rhs[step, X, piece]
        flat = flattened(step, part)
        for dy in (-1, 1):
            for n, base in enumerate(lines(part, dy, False)):
                y_send[step, part, (dy + 1) // 2, n] = flat[pl.ds(base, slab, stride=TALL), :]
        w = 1 if part == 0 else DEEP - 1
        for dx in (-1, 1):
            for dy in (-1, 1):
                m = (dx + 1) + (dy + 1) // 2
                x, y = rim(dx, w, slab)[0], ROW + rim(dy, w, rows)[0]
                if part == 0:
                    for f in range(2):
                        c_send[step, part, m, f:f + 1] = ext[step, f, 2 + x, y:y + 1]
                else:
                    for n in range(w):
                        c_send[step, part, m, w * n:w * n + w] = rhs[step, DEEP + x + n, y:y + w]

    def start_all(step, part):
        for dx in (-1, 1):
            @pl.when(ends[dx])
            def _():
                for k in range(ngy):
                    shear_message(step, part, dx, k).start()
        for dx in (-1, 1):
            @pl.when(has[dx])
            def _():
                for dy in (0, -1, 1):
                    messages(step, part, dx, dy).start()
        for dy in (-1, 1):
            messages(step, part, 0, dy).start()

    def sheared(step, part, dx):
        span = rows * ngy
        shift = span - offsets[step] if dx > 0 else offsets[step]
        start = lax.rem(gy * rows + shift + (span - ROW), span)
        block, within = lax.div(start, 8), lax.rem(start, 8)
        blocks = [lax.rem(block + c, span // 8) for c in range(TALL // 8 + 1)]
        for n in range(DEEP):
            tall = jnp.concatenate([shear_recv[2 * step + part][n, at] for at in blocks], axis=0)
            plane = pltpu.roll(tall, TALL + 8 - within, 0)[:TALL]
            if part == 0:
                f, X = field_planes(dx, True)[n]
                ext[step, f, X] = plane
            else:
                rhs[step, DEEP + rim(dx, DEEP, slab)[1] + n] = plane

    def unpack_x(step, part, dx):
        m = (dx + 1) // 2
        for n in range(DEEP):
            if part == 0:
                f, X = field_planes(dx, True)[n]
            else:
                X = DEEP + rim(dx, DEEP, slab)[1] + n
            for c in range(rows // 8):
                piece = slice(ROW + 8 * c, ROW + 8 * c + 8)
                value = x_recv[step, part, m, n, c]
                if part == 0:
                    ext[step, f, X, piece] = value
                else:
                    rhs[step, X, piece] = value

    def unpack_corner(step, part, dx, dy):
        m = (dx + 1) + (dy + 1) // 2
        w = 1 if part == 0 else DEEP - 1
        x, y = rim(dx, w, slab)[1], ROW + rim(dy, w, rows)[1]
        if part == 0:
            for f in range(2):
                ext[step, f, 2 + x, y:y + 1] = c_recv[step, part, m, f:f + 1]
        else:
            for n in range(w):
                rhs[step, DEEP + x + n, y:y + w] = c_recv[step, part, m, w * n:w * n + w]

    def arrive_all(step, part):
        flat = flattened(step, part)
        for dy in (-1, 1):
            messages(step, part, 0, dy).wait_recv()
            for n, base in enumerate(lines(part, dy, True)):
                flat[pl.ds(base, slab, stride=TALL), :] = y_recv[step, part, (dy + 1) // 2, n]
        for dx in (-1, 1):
            @pl.when(has[-dx])
            def _():
                messages(step, part, dx, 0).wait_recv()
                unpack_x(step, part, dx)
                for dy in (-1, 1):
                    messages(step, part, dx, dy).wait_recv()
                    unpack_corner(step, part, dx, dy)
        for dx in (-1, 1):
            @pl.when(ends[-dx])
            def _():
                for k in range(ngy):
                    shear_arrival(step, part, -dx, k).wait_recv()
                sheared(step, part, dx)

    def sent_all(step, part):
        for dy in (-1, 1):
            messages(step, part, 0, dy).wait_send()
        for dx in (-1, 1):
            @pl.when(has[dx])
            def _():
                for dy in (0, -1, 1):
                    messages(step, part, dx, dy).wait_send()

            @pl.when(ends[dx])
            def _():
                for k in range(ngy):
                    shear_message(step, part, dx, k).wait_send()

    half = -0.5 * time_step
    keep = 1.0 - 6.0 * time_step * viscosity
    spread = time_step * viscosity

    def move(c, parts, hu, hv, hw):
        total, ddx, ddy, ddz = parts
        return (keep * c + spread * total) + (hu * ddx + hv * ddy + hw * ddz)

    def mean_flow(x):
        return rate * (x.astype(jnp.float32) + (0.5 - total_x / 2.0))

    lo, hi = ROW, ROW + rows

    def provisional(step):
        e = ext.at[step]

        def around(f, X):
            c = e[f, X, lo:hi]
            return c, stencil(c, e[f, X - 1, lo:hi], e[f, X + 1, lo:hi],
                              e[f, X, lo - 1:hi - 1], e[f, X, lo + 1:hi + 1])

        def speeds(X):
            flow = mean_flow(lax.rem(gx * slab + (X - 2) + total_x, total_x))
            u, v, w = e[0, X, lo:hi], e[1, X, lo:hi], e[2, X, lo:hi]
            return u, half * u, half * (v + flow), half * w

        def plane(i, _):
            X = i + 2
            u, hu, hv, hw = speeds(X)
            for f in range(4):
                c, parts = around(f, X)
                value = move(c, parts, hu, hv, hw)
                if f == 1:
                    value = value - (time_step * rate) * u
                if f == 3:
                    value = value - time_step * u
                prov[f, i + 1, lo:hi] = value
            return 0

        loop(0, slab, plane)
        for X in (1, slab + 2):
            u, hu, hv, hw = speeds(X)
            c, parts = around(0, X)
            prov[0, X - 1, lo:hi] = move(c, parts, hu, hv, hw)
        flat = e.reshape(4 * (slab + 4) * TALL, 128)
        into = prov.reshape(4 * (slab + 2) * TALL, 128)
        place = gx * slab + lax.broadcasted_iota(jnp.int32, (slab, 128), 0)
        flow = mean_flow(place)
        for y in (-1, rows):
            def line(f, x, yy):
                return flat[pl.ds((f * (slab + 4) + 2 + x) * TALL + ROW + yy, slab, stride=TALL), :]

            u, c, w = line(0, 0, y), line(1, 0, y), line(2, 0, y)
            parts = stencil(c, line(1, -1, y), line(1, 1, y), line(1, 0, y - 1), line(1, 0, y + 1))
            value = move(c, parts, half * u, half * (c + flow), half * w) - (time_step * rate) * u
            into[pl.ds((slab + 2 + 1) * TALL + ROW + y, slab, stride=TALL), :] = value

    def divergence(step):
        scale = 0.5 / (6.0 * time_step)

        def plane(i, _):
            dx = prov[0, i + 2, lo:hi] - prov[0, i, lo:hi]
            dy = prov[1, i + 1, lo + 1:hi + 1] - prov[1, i + 1, lo - 1:hi - 1]
            w = prov[2, i + 1, lo:hi]
            rhs[step, DEEP + i, lo:hi] = scale * (dx + dy + (across(w, -1) - across(w, 1)))
            return 0

        loop(0, slab, plane)

    def relax(step):
        r = rhs.at[step]
        top, bottom = ROW - RELAX, ROW + rows + RELAX

        def first(X, _):
            c = r[X, top:bottom]
            total = stencil(c, r[X - 1, top:bottom], r[X + 1, top:bottom],
                            r[X, top - 1:bottom - 1], r[X, top + 1:bottom + 1])[0]
            press[0, X, top:bottom] = -(total * (1.0 / 6.0) + c)
            return 0

        loop(1, slab + 2 * DEEP - 1, first)
        for k in range(1, RELAX):
            old, new = press.at[k - 1], press.at[k]

            def sweep(X, _):
                c = old[X, top:bottom]
                total = stencil(c, old[X - 1, top:bottom], old[X + 1, top:bottom],
                                old[X, top - 1:bottom - 1], old[X, top + 1:bottom + 1])[0]
                new[X, top:bottom] = total * (1.0 / 6.0) - r[X, top:bottom]
                return 0

            loop(1 + k, slab + 2 * DEEP - 1 - k, sweep)

    def project(step, store):
        p = press.at[RELAX - 1]

        def plane(i, _):
            X = DEEP + i
            c = p[X, lo:hi]
            store(0, i, prov[0, i + 1, lo:hi] + half * (p[X + 1, lo:hi] - p[X - 1, lo:hi]))
            store(1, i, prov[1, i + 1, lo:hi] + half * (p[X, lo + 1:hi + 1] - p[X, lo - 1:hi - 1]))
            store(2, i, prov[2, i + 1, lo:hi] + half * (across(c, -1) - across(c, 1)))
            store(3, i, prov[3, i + 1, lo:hi])
            return 0

        loop(0, slab, plane)

    fetch.wait()
    for step in range(steps):
        pack(step, 0)
        if step == 0:
            inner = jnp.logical_and(gx > 0, gx < ngx - 1)

            @pl.when(inner)
            def _():
                pl.semaphore_wait(barrier, 8)

            @pl.when(jnp.logical_not(inner))
            def _():
                pl.semaphore_wait(barrier, 5 + ngy)

        start_all(step, 0)
        arrive_all(step, 0)
        provisional(step)
        divergence(step)
        pack(step, 1)
        start_all(step, 1)
        arrive_all(step, 1)
        relax(step)
        if step < steps - 1:
            def store(f, i, value, step=step):
                ext[step + 1, f, i + 2, lo:hi] = value
        else:
            def store(f, i, value):
                final[f, i] = value
        project(step, store)

    give = pltpu.make_async_copy(final, out, local_sem.at[1])
    give.start()
    for step in range(steps):
        for part in range(2):
            sent_all(step, part)
    give.wait()


def local(ngx, ngy, state, offsets):
    steps = offsets.shape[0]
    fields, slab, rows, depth = state.shape
    f32 = jnp.float32
    return pl.pallas_call(
        functools.partial(kernel, ngx, ngy, steps),
        out_shape=jax.ShapeDtypeStruct(state.shape, f32),
        in_specs=[pl.BlockSpec(memory_space=pltpu.SMEM), pl.BlockSpec(memory_space=pl.ANY)],
        out_specs=pl.BlockSpec(memory_space=pl.ANY),
        scratch_shapes=[
            pltpu.VMEM((steps, fields, slab + 4, TALL, depth), f32),
            pltpu.VMEM((fields, slab + 2, TALL, depth), f32),
            pltpu.VMEM((steps, slab + 2 * DEEP, TALL, depth), f32),
            pltpu.VMEM((RELAX, slab + 2 * DEEP, TALL, depth), f32),
            pltpu.VMEM(state.shape, f32),
            pltpu.VMEM((steps, 2, 2, DEEP, rows // 8, 8, depth), f32),
            pltpu.VMEM((steps, 2, 2, DEEP, rows // 8, 8, depth), f32),
            pltpu.VMEM((steps, 2, 2, DEEP, slab, depth), f32),
            pltpu.VMEM((steps, 2, 2, DEEP, slab, depth), f32),
            pltpu.VMEM((steps, 2, 4, 16, depth), f32),
            pltpu.VMEM((steps, 2, 4, 16, depth), f32),
            pltpu.SemaphoreType.DMA((steps, 2, 8)),
            pltpu.SemaphoreType.DMA((steps, 2, 8)),
            pltpu.SemaphoreType.DMA((steps, 2, ngy)),
            pltpu.SemaphoreType.DMA((steps, 2, ngy)),
            pltpu.SemaphoreType.DMA((2,)),
        ] + [pltpu.VMEM((DEEP, ngy * rows // 8, 8, depth), f32)] * (2 * steps),
        compiler_params=pltpu.CompilerParams(
            collective_id=0, has_side_effects=True, vmem_limit_bytes=32 * 1024 * 1024
        ),
    )(offsets, state)


def solution(mesh):
    in_specs = (P(None, "gx", "gy", None), P())
    out_specs = P(None, "gx", "gy", None)
    body = functools.partial(local, mesh.shape["gx"], mesh.shape["gy"])
    return jax.shard_map(body, mesh=mesh, in_specs=in_specs, out_specs=out_specs, check_vma=False)
```

```python
import functools

import jax
import jax.numpy as jnp
from jax import lax
from jax.experimental import pallas as pl
from jax.experimental.pallas import tpu as pltpu
from jax.sharding import PartitionSpec as P

RELAX = 4
DEEP = RELAX + 1

time_step = 0.2
viscosity = 0.1

MESH = pl.DeviceIdType.MESH
ROW = 8
TALL = 32


def across(x, shift):
    return pltpu.roll(x, shift % x.shape[-1], x.ndim - 1)


def stencil(c, xm, xp, ym, yp):
    zp, zm = across(c, -1), across(c, 1)
    total = (xp + xm) + (yp + ym) + (zp + zm)
    return total, xp - xm, yp - ym, zp - zm


def kernel(ngx, ngy, steps, offsets_in, state, out, ext, prov, rhs, press,
           x_send, x_recv, y_send, y_recv, c_send, c_recv, send_sem, recv_sem, shear_out, shear_in, local_sem, offsets, *shear_recv):
    slab, rows = state.shape[1], state.shape[2]
    gx, gy = lax.axis_index("gx"), lax.axis_index("gy")
    below, above = lax.rem(gx + ngx - 1, ngx), lax.rem(gx + 1, ngx)
    left, right = lax.rem(gy + ngy - 1, ngy), lax.rem(gy + 1, ngy)
    at_x = {-1: below, 0: gx, 1: above}
    at_y = {-1: left, 0: gy, 1: right}
    has = {-1: gx > 0, 1: gx < ngx - 1}
    ends = {-1: gx == 0, 1: gx == ngx - 1}
    far = {-1: ngx - 1, 1: 0}
    total_x = slab * ngx
    rate = 2.0 / total_x
    own = pl.ds(ROW, rows)

    fetch = pltpu.make_async_copy(state, ext.at[0, :, pl.ds(2, slab), own, :], local_sem.at[0])
    fetch.start()
    fetch_offsets = pltpu.make_async_copy(offsets_in, offsets, local_sem.at[2])
    fetch_offsets.start()

    barrier = pltpu.get_barrier_semaphore()

    def greet(x, y):
        pl.semaphore_signal(barrier, inc=1, device_id=(x, y), device_id_type=MESH)

    for dy in (-1, 1):
        greet(gx, at_y[dy])
    for dx in (-1, 1):
        @pl.when(has[dx])
        def _():
            for dy in (-1, 0, 1):
                greet(at_x[dx], at_y[dy])

        @pl.when(ends[dx])
        def _():
            for k in range(ngy):
                greet(far[dx], k)

    def remote(src, dst, send, recv, x, y):
        return pltpu.make_async_remote_copy(
            src_ref=src, dst_ref=dst, send_sem=send, recv_sem=recv,
            device_id=(x, y), device_id_type=MESH)

    def rim(side, width, size):
        return (0, size) if side < 0 else (size - width, -width)

    def messages(step, part, dx, dy):
        dev = at_x[dx], at_y[dy]
        if dx == 0:
            n = m = (dy + 1) // 2
            src, dst = y_send.at[step, part, m], y_recv.at[step, part, m]
        elif dy == 0:
            m = (dx + 1) // 2
            n = 2 + m
            src, dst = x_send.at[step, part, m], x_recv.at[step, part, m]
        else:
            m = (dx + 1) + (dy + 1) // 2
            n = 4 + m
            size = pl.ds(0, 8 if part == 0 else 16)
            src, dst = c_send.at[step, part, m, size, :], c_recv.at[step, part, m, size, :]
        return remote(src, dst, send_sem.at[step, part, n], recv_sem.at[step, part, n], *dev)

    def shear_part(kind, dx):
        if kind == 0:
            return 0, DEEP
        deep = DEEP - 2
        if kind == 1:
            return (2 if dx < 0 else 0), deep
        return (0 if dx < 0 else deep), 2

    def shear_slot(step, kind, k):
        return shear_recv[3 * step + kind].at[:, pl.ds(k * (rows // 8), rows // 8), :, :]

    def shear_message(step, kind, dx, k):
        first, count = shear_part(kind, dx)
        src = x_send.at[step, min(kind, 1), (dx + 1) // 2, pl.ds(first, count)]
        return remote(src, shear_slot(step, kind, gy),
                      shear_out.at[step, kind, k], shear_in.at[step, kind, gy], far[dx], k)

    def shear_arrival(step, kind, dx, k):
        slot = shear_slot(step, kind, k)
        return remote(slot, slot, shear_out.at[step, kind, k], shear_in.at[step, kind, k], far[dx], k)

    def field_planes(dx, ghost):
        s2, d2 = rim(dx, 2, slab)
        s1, d1 = rim(dx, 1, slab)
        p2, p1 = (d2, d1) if ghost else (s2, s1)
        return [(0, 2 + p2), (0, 3 + p2), (1, 2 + p1), (2, 2 + p1), (3, 2 + p1)]

    def lines(part, dy, ghost):
        if part == 0:
            s2, d2 = rim(dy, 2, rows)
            s1, d1 = rim(dy, 1, rows)
            p2, p1 = (d2, d1) if ghost else (s2, s1)
            return [(f * (slab + 4) + 2) * TALL + ROW + y
                    for f, y in ((1, p2), (1, p2 + 1), (0, p1), (2, p1), (3, p1))]
        s, d = rim(dy, DEEP, rows)
        return [DEEP * TALL + ROW + (d if ghost else s) + k for k in range(DEEP)]

    def flattened(step, part):
        if part == 0:
            return ext.at[step].reshape(4 * (slab + 4) * TALL, 128)
        return rhs.at[step].reshape((slab + 2 * DEEP) * TALL, 128)

    def pack_x(step, part, dx, first=0, count=DEEP):
        m = (dx + 1) // 2
        for n in range(first, first + count):
            if part == 0:
                f, X = field_planes(dx, False)[n]
            else:
                X = DEEP + rim(dx, DEEP, slab)[0] + n
            for c in range(rows // 8):
                piece = slice(ROW + 8 * c, ROW + 8 * c + 8)
                x_send[step, part, m, n, c] = ext[step, f, X, piece] if part == 0 else rhs[step, X, piece]

    def pack_y(step, part, dy):
        flat = flattened(step, part)
        for n, base in enumerate(lines(part, dy, False)):
            y_send[step, part, (dy + 1) // 2, n] = flat[pl.ds(base, slab, stride=TALL), :]

    def pack_corner(step, part, dx, dy):
        w = 1 if part == 0 else DEEP - 1
        m = (dx + 1) + (dy + 1) // 2
        x, y = rim(dx, w, slab)[0], ROW + rim(dy, w, rows)[0]
        if part == 0:
            for f in range(2):
                c_send[step, part, m, f:f + 1] = ext[step, f, 2 + x, y:y + 1]
        else:
            for n in range(w):
                c_send[step, part, m, w * n:w * n + w] = rhs[step, DEEP + x + n, y:y + w]

    def start_shear(step, kind):
        for dx in (-1, 1):
            @pl.when(ends[dx])
            def _():
                if kind > 0:
                    pack_x(step, 1, dx, *shear_part(kind, dx))
                else:
                    pack_x(step, 0, dx)
                for k in range(ngy):
                    shear_message(step, kind, dx, k).start()

    def start_x(step, part):
        for dx in (-1, 1):
            @pl.when(has[dx])
            def _():
                pack_x(step, part, dx)
                messages(step, part, dx, 0).start()
                for dy in (-1, 1):
                    pack_corner(step, part, dx, dy)
                    messages(step, part, dx, dy).start()

    def start_y(step, part):
        for dy in (-1, 1):
            pack_y(step, part, dy)
            messages(step, part, 0, dy).start()

    def sheared(step, kind, dx):
        span = rows * ngy
        shift = span - offsets[step] if dx > 0 else offsets[step]
        start = lax.rem(gy * rows + shift + (span - ROW), span)
        block, within = lax.div(start, 8), lax.rem(start, 8)
        blocks = [lax.rem(block + c, span // 8) for c in range(TALL // 8 + 1)]
        first, count = shear_part(kind, dx)
        for n in range(first, first + count):
            tall = jnp.concatenate([shear_recv[3 * step + kind][n - first, at] for at in blocks], axis=0)
            plane = pltpu.roll(tall, TALL + 8 - within, 0)[:TALL]
            if kind == 0:
                f, X = field_planes(dx, True)[n]
                ext[step, f, X] = plane
            else:
                rhs[step, DEEP + rim(dx, DEEP, slab)[1] + n] = plane

    def unpack_x(step, part, dx):
        m = (dx + 1) // 2
        for n in range(DEEP):
            if part == 0:
                f, X = field_planes(dx, True)[n]
            else:
                X = DEEP + rim(dx, DEEP, slab)[1] + n
            for c in range(rows // 8):
                piece = slice(ROW + 8 * c, ROW + 8 * c + 8)
                value = x_recv[step, part, m, n, c]
                if part == 0:
                    ext[step, f, X, piece] = value
                else:
                    rhs[step, X, piece] = value

    def unpack_corner(step, part, dx, dy):
        m = (dx + 1) + (dy + 1) // 2
        w = 1 if part == 0 else DEEP - 1
        x, y = rim(dx, w, slab)[1], ROW + rim(dy, w, rows)[1]
        if part == 0:
            for f in range(2):
                ext[step, f, 2 + x, y:y + 1] = c_recv[step, part, m, f:f + 1]
        else:
            for n in range(w):
                rhs[step, DEEP + x + n, y:y + w] = c_recv[step, part, m, w * n:w * n + w]

    def arrive_y(step, part):
        flat = flattened(step, part)
        for dy in (-1, 1):
            messages(step, part, 0, dy).wait_recv()
            for n, base in enumerate(lines(part, dy, True)):
                flat[pl.ds(base, slab, stride=TALL), :] = y_recv[step, part, (dy + 1) // 2, n]

    def arrive_x(step, part):
        for dx in (-1, 1):
            @pl.when(has[-dx])
            def _():
                messages(step, part, dx, 0).wait_recv()
                unpack_x(step, part, dx)
                for dy in (-1, 1):
                    messages(step, part, dx, dy).wait_recv()
                    unpack_corner(step, part, dx, dy)
        for dx in (-1, 1):
            @pl.when(ends[-dx])
            def _():
                for kind in ((0,) if part == 0 else (1, 2)):
                    for k in range(ngy):
                        shear_arrival(step, kind, -dx, k).wait_recv()
                    sheared(step, kind, dx)

    def sent_all(step):
        for part in range(2):
            for dy in (-1, 1):
                messages(step, part, 0, dy).wait_send()
            for dx in (-1, 1):
                @pl.when(has[dx])
                def _():
                    for dy in (0, -1, 1):
                        messages(step, part, dx, dy).wait_send()
        for dx in (-1, 1):
            @pl.when(ends[dx])
            def _():
                for kind in range(3):
                    for k in range(ngy):
                        shear_message(step, kind, dx, k).wait_send()

    half = -0.5 * time_step
    keep = 1.0 - 6.0 * time_step * viscosity
    spread = time_step * viscosity

    def move(c, parts, hu, hv, hw):
        total, ddx, ddy, ddz = parts
        return (keep * c + spread * total) + (hu * ddx + hv * ddy + hw * ddz)

    def mean_flow(x):
        return rate * (x.astype(jnp.float32) + (0.5 - total_x / 2.0))

    lo, hi = ROW, ROW + rows

    def speeds(step, X):
        e = ext.at[step]
        flow = mean_flow(lax.rem(gx * slab + (X - 2) + total_x, total_x))
        u, v, w = e[0, X, lo:hi], e[1, X, lo:hi], e[2, X, lo:hi]
        return u, half * u, half * (v + flow), half * w

    def around(step, f, X):
        e = ext.at[step]
        c = e[f, X, lo:hi]
        return c, stencil(c, e[f, X - 1, lo:hi], e[f, X + 1, lo:hi],
                          e[f, X, lo - 1:hi - 1], e[f, X, lo + 1:hi + 1])

    def provisional(step, planes):
        for i in planes:
            X = i + 2
            u, hu, hv, hw = speeds(step, X)
            for f in range(4):
                c, parts = around(step, f, X)
                value = move(c, parts, hu, hv, hw)
                if f == 1:
                    value = value - (time_step * rate) * u
                if f == 3:
                    value = value - time_step * u
                prov[f, i + 1, lo:hi] = value

    def provisional_x_ghosts(step):
        for X in (1, slab + 2):
            u, hu, hv, hw = speeds(step, X)
            c, parts = around(step, 0, X)
            prov[0, X - 1, lo:hi] = move(c, parts, hu, hv, hw)

    def provisional_y_ghosts(step):
        flat = flattened(step, 0)
        into = prov.reshape(4 * (slab + 2) * TALL, 128)
        place = gx * slab + lax.broadcasted_iota(jnp.int32, (slab, 128), 0)
        flow = mean_flow(place)
        for y in (-1, rows):
            def line(f, x, yy):
                return flat[pl.ds((f * (slab + 4) + 2 + x) * TALL + ROW + yy, slab, stride=TALL), :]

            u, c, w = line(0, 0, y), line(1, 0, y), line(2, 0, y)
            parts = stencil(c, line(1, -1, y), line(1, 1, y), line(1, 0, y - 1), line(1, 0, y + 1))
            value = move(c, parts, half * u, half * (c + flow), half * w) - (time_step * rate) * u
            into[pl.ds((slab + 2 + 1) * TALL + ROW + y, slab, stride=TALL), :] = value

    def divergence(step, planes):
        scale = 0.5 / (6.0 * time_step)
        for i in planes:
            dx = prov[0, i + 2, lo:hi] - prov[0, i, lo:hi]
            dy = prov[1, i + 1, lo + 1:hi + 1] - prov[1, i + 1, lo - 1:hi - 1]
            w = prov[2, i + 1, lo:hi]
            rhs[step, DEEP + i, lo:hi] = scale * (dx + dy + (across(w, -1) - across(w, 1)))

    def relax(step, k, planes):
        r = rhs.at[step]
        top, bottom = ROW - RELAX, ROW + rows + RELAX
        old, new = (press.at[k - 1] if k else r), press.at[k]
        for x in planes:
            X = DEEP + x
            c = old[X, top:bottom]
            total = stencil(c, old[X - 1, top:bottom], old[X + 1, top:bottom],
                            old[X, top - 1:bottom - 1], old[X, top + 1:bottom + 1])[0]
            if k == 0:
                new[X, top:bottom] = -(total * (1.0 / 6.0) + c)
            else:
                new[X, top:bottom] = total * (1.0 / 6.0) - r[X, top:bottom]

    def project(step, planes):
        p = press.at[RELAX - 1]

        def store(f, i, value):
            if step < steps - 1:
                ext[step + 1, f, i + 2, lo:hi] = value
            else:
                out[f, i] = value

        for i in planes:
            X = DEEP + i
            c = p[X, lo:hi]
            store(0, i, prov[0, i + 1, lo:hi] + half * (p[X + 1, lo:hi] - p[X - 1, lo:hi]))
            store(1, i, prov[1, i + 1, lo:hi] + half * (p[X, lo + 1:hi + 1] - p[X, lo - 1:hi - 1]))
            store(2, i, prov[2, i + 1, lo:hi] + half * (across(c, -1) - across(c, 1)))
            store(3, i, prov[3, i + 1, lo:hi])

    fetch.wait()
    inner = jnp.logical_and(gx > 0, gx < ngx - 1)

    @pl.when(inner)
    def _():
        pl.semaphore_wait(barrier, 8)

    @pl.when(jnp.logical_not(inner))
    def _():
        pl.semaphore_wait(barrier, 5 + ngy)

    for step in range(steps):
        if step == 0:
            start_shear(step, 0)
            start_x(step, 0)
            start_y(step, 0)
            fetch_offsets.wait()
        arrive_y(step, 0)
        provisional(step, range(1, slab - 1))
        provisional_y_ghosts(step)
        divergence(step, range(2, slab - 2))
        start_shear(step, 1)
        arrive_x(step, 0)
        provisional(step, (0, slab - 1))
        provisional_x_ghosts(step)
        provisional_y_ghosts(step)
        divergence(step, (0, 1, slab - 2, slab - 1))
        start_shear(step, 2)
        start_x(step, 1)
        start_y(step, 1)
        arrive_y(step, 1)
        for k in range(RELAX):
            relax(step, k, range(k + 1, slab - k - 1))
        early = range(RELAX + 1, slab - RELAX - 1)
        project(step, early)
        arrive_x(step, 1)
        for k in range(RELAX):
            relax(step, k, range(k - RELAX, k + 1))
            relax(step, k, range(slab - k - 1, slab + RELAX - k))
        ends_first = (0, 1, slab - 2, slab - 1)
        project(step, ends_first)
        if step < steps - 1:
            start_shear(step + 1, 0)
            start_x(step + 1, 0)
        project(step, [i for i in range(slab) if i not in ends_first and i not in early])
        if step < steps - 1:
            start_y(step + 1, 0)

    for step in range(steps):
        sent_all(step)


def local(ngx, ngy, state, offsets):
    steps = offsets.shape[0]
    fields, slab, rows, depth = state.shape
    f32 = jnp.float32
    return pl.pallas_call(
        functools.partial(kernel, ngx, ngy, steps),
        out_shape=jax.ShapeDtypeStruct(state.shape, f32),
        in_specs=[pl.BlockSpec(memory_space=pl.ANY), pl.BlockSpec(memory_space=pl.ANY)],
        out_specs=pl.BlockSpec(memory_space=pltpu.VMEM),
        scratch_shapes=[
            pltpu.VMEM((steps, fields, slab + 4, TALL, depth), f32),
            pltpu.VMEM((fields, slab + 2, TALL, depth), f32),
            pltpu.VMEM((steps, slab + 2 * DEEP, TALL, depth), f32),
            pltpu.VMEM((RELAX, slab + 2 * DEEP, TALL, depth), f32),
            pltpu.VMEM((steps, 2, 2, DEEP, rows // 8, 8, depth), f32),
            pltpu.VMEM((steps, 2, 2, DEEP, rows // 8, 8, depth), f32),
            pltpu.VMEM((steps, 2, 2, DEEP, slab, depth), f32),
            pltpu.VMEM((steps, 2, 2, DEEP, slab, depth), f32),
            pltpu.VMEM((steps, 2, 4, 16, depth), f32),
            pltpu.VMEM((steps, 2, 4, 16, depth), f32),
            pltpu.SemaphoreType.DMA((steps, 2, 8)),
            pltpu.SemaphoreType.DMA((steps, 2, 8)),
            pltpu.SemaphoreType.DMA((steps, 3, ngy)),
            pltpu.SemaphoreType.DMA((steps, 3, ngy)),
            pltpu.SemaphoreType.DMA((3,)),
            pltpu.SMEM((steps,), jnp.int32),
        ] + [pltpu.VMEM((count, ngy * rows // 8, 8, depth), f32) for count in (DEEP, DEEP - 2, 2)] * steps,
        compiler_params=pltpu.CompilerParams(
            collective_id=0, has_side_effects=True, vmem_limit_bytes=32 * 1024 * 1024
        ),
    )(offsets, state)


def solution(mesh):
    in_specs = (P(None, "gx", "gy", None), P())
    out_specs = P(None, "gx", "gy", None)
    body = functools.partial(local, mesh.shape["gx"], mesh.shape["gy"])
    return jax.shard_map(body, mesh=mesh, in_specs=in_specs, out_specs=out_specs, check_vma=False)
```

```python
import functools

import jax
import jax.numpy as jnp
from jax import lax
from jax.experimental import pallas as pl
from jax.experimental.pallas import tpu as pltpu
from jax.sharding import PartitionSpec as P

RELAX = 4
DEEP = RELAX + 1

time_step = 0.2
viscosity = 0.1

MESH = pl.DeviceIdType.MESH
ROW = 8
TALL = 32


def across(x, shift):
    return pltpu.roll(x, shift % x.shape[-1], x.ndim - 1)


def stencil(c, xm, xp, ym, yp):
    zp, zm = across(c, -1), across(c, 1)
    total = (xp + xm) + (yp + ym) + (zp + zm)
    return total, xp - xm, yp - ym, zp - zm


def kernel(ngx, ngy, steps, offsets_in, state, out, ext, prov, rhs, press,
           x_send, x_recv, y_send, y_recv, c_send, c_recv, send_sem, recv_sem, shear_out, shear_in, local_sem, offsets, *shear_recv):
    slab, rows = state.shape[1], state.shape[2]
    gx, gy = lax.axis_index("gx"), lax.axis_index("gy")
    below, above = lax.rem(gx + ngx - 1, ngx), lax.rem(gx + 1, ngx)
    left, right = lax.rem(gy + ngy - 1, ngy), lax.rem(gy + 1, ngy)
    at_x = {-1: below, 0: gx, 1: above}
    at_y = {-1: left, 0: gy, 1: right}
    has = {-1: gx > 0, 1: gx < ngx - 1}
    ends = {-1: gx == 0, 1: gx == ngx - 1}
    far = {-1: ngx - 1, 1: 0}
    total_x = slab * ngx
    rate = 2.0 / total_x
    own = pl.ds(ROW, rows)

    fetch = pltpu.make_async_copy(state, ext.at[0, :, pl.ds(2, slab), own, :], local_sem.at[0])
    fetch.start()
    fetch_offsets = pltpu.make_async_copy(offsets_in, offsets, local_sem.at[2])
    fetch_offsets.start()

    barrier = pltpu.get_barrier_semaphore()

    def greet(x, y):
        pl.semaphore_signal(barrier, inc=1, device_id=(x, y), device_id_type=MESH)

    for dy in (-1, 1):
        greet(gx, at_y[dy])
    for dx in (-1, 1):
        @pl.when(has[dx])
        def _():
            for dy in (-1, 0, 1):
                greet(at_x[dx], at_y[dy])

        @pl.when(ends[dx])
        def _():
            for k in range(ngy):
                greet(far[dx], k)

    def remote(src, dst, send, recv, x, y):
        return pltpu.make_async_remote_copy(
            src_ref=src, dst_ref=dst, send_sem=send, recv_sem=recv,
            device_id=(x, y), device_id_type=MESH)

    def rim(side, width, size):
        return (0, size) if side < 0 else (size - width, -width)

    def messages(step, part, dx, dy):
        dev = at_x[dx], at_y[dy]
        if dx == 0:
            n = m = (dy + 1) // 2
            src, dst = y_send.at[step, part, m], y_recv.at[step, part, m]
        elif dy == 0:
            m = (dx + 1) // 2
            n = 2 + m
            src, dst = x_send.at[step, part, m], x_recv.at[step, part, m]
        else:
            m = (dx + 1) + (dy + 1) // 2
            n = 4 + m
            size = pl.ds(0, 8 if part == 0 else 16)
            src, dst = c_send.at[step, part, m, size, :], c_recv.at[step, part, m, size, :]
        return remote(src, dst, send_sem.at[step, part, n], recv_sem.at[step, part, n], *dev)

    def shear_part(kind, dx):
        if kind == 0:
            return 0, DEEP
        deep = DEEP - 2
        if kind == 1:
            return (2 if dx < 0 else 0), deep
        return (0 if dx < 0 else deep), 2

    def shear_slot(step, kind, k):
        return shear_recv[3 * step + kind].at[:, pl.ds(k * (rows // 8), rows // 8), :, :]

    def shear_message(step, kind, dx, k):
        first, count = shear_part(kind, dx)
        src = x_send.at[step, min(kind, 1), (dx + 1) // 2, pl.ds(first, count)]
        return remote(src, shear_slot(step, kind, gy),
                      shear_out.at[step, kind, k], shear_in.at[step, kind, gy], far[dx], k)

    def shear_arrival(step, kind, dx, k):
        slot = shear_slot(step, kind, k)
        return remote(slot, slot, shear_out.at[step, kind, k], shear_in.at[step, kind, k], far[dx], k)

    def field_planes(dx, ghost):
        s2, d2 = rim(dx, 2, slab)
        s1, d1 = rim(dx, 1, slab)
        p2, p1 = (d2, d1) if ghost else (s2, s1)
        return [(0, 2 + p2), (0, 3 + p2), (1, 2 + p1), (2, 2 + p1), (3, 2 + p1)]

    def lines(part, dy, ghost):
        if part == 0:
            s2, d2 = rim(dy, 2, rows)
            s1, d1 = rim(dy, 1, rows)
            p2, p1 = (d2, d1) if ghost else (s2, s1)
            return [(f * (slab + 4) + 2) * TALL + ROW + y
                    for f, y in ((1, p2), (1, p2 + 1), (0, p1), (2, p1), (3, p1))]
        s, d = rim(dy, DEEP, rows)
        return [DEEP * TALL + ROW + (d if ghost else s) + k for k in range(DEEP)]

    def flattened(step, part):
        if part == 0:
            return ext.at[step].reshape(4 * (slab + 4) * TALL, 128)
        return rhs.at[step].reshape((slab + 2 * DEEP) * TALL, 128)

    def pack_x(step, part, dx, first=0, count=DEEP):
        m = (dx + 1) // 2
        for n in range(first, first + count):
            if part == 0:
                f, X = field_planes(dx, False)[n]
            else:
                X = DEEP + rim(dx, DEEP, slab)[0] + n
            for c in range(rows // 8):
                piece = slice(ROW + 8 * c, ROW + 8 * c + 8)
                x_send[step, part, m, n, c] = ext[step, f, X, piece] if part == 0 else rhs[step, X, piece]

    def pack_y(step, part, dy):
        flat = flattened(step, part)
        for n, base in enumerate(lines(part, dy, False)):
            y_send[step, part, (dy + 1) // 2, n] = flat[pl.ds(base, slab, stride=TALL), :]

    def pack_corner(step, part, dx, dy):
        w = 1 if part == 0 else DEEP - 1
        m = (dx + 1) + (dy + 1) // 2
        x, y = rim(dx, w, slab)[0], ROW + rim(dy, w, rows)[0]
        if part == 0:
            for f in range(2):
                c_send[step, part, m, f:f + 1] = ext[step, f, 2 + x, y:y + 1]
        else:
            for n in range(w):
                c_send[step, part, m, w * n:w * n + w] = rhs[step, DEEP + x + n, y:y + w]

    def start_shear(step, kind):
        for dx in (-1, 1):
            @pl.when(ends[dx])
            def _():
                if kind > 0:
                    pack_x(step, 1, dx, *shear_part(kind, dx))
                else:
                    pack_x(step, 0, dx)
                for away in range(ngy):
                    shear_message(step, kind, dx, lax.rem(gy + away, ngy)).start()

    def start_x(step, part):
        for dx in (-1, 1):
            @pl.when(has[dx])
            def _():
                pack_x(step, part, dx)
                messages(step, part, dx, 0).start()
                for dy in (-1, 1):
                    pack_corner(step, part, dx, dy)
                    messages(step, part, dx, dy).start()

    def start_y(step, part):
        for dy in (-1, 1):
            pack_y(step, part, dy)
            messages(step, part, 0, dy).start()

    def sheared(step, kind, dx):
        span = rows * ngy
        shift = span - offsets[step] if dx > 0 else offsets[step]
        start = lax.rem(gy * rows + shift + (span - ROW), span)
        block, within = lax.div(start, 8), lax.rem(start, 8)
        blocks = [lax.rem(block + c, span // 8) for c in range(TALL // 8 + 1)]
        first, count = shear_part(kind, dx)
        for n in range(first, first + count):
            tall = jnp.concatenate([shear_recv[3 * step + kind][n - first, at] for at in blocks], axis=0)
            plane = pltpu.roll(tall, TALL + 8 - within, 0)[:TALL]
            if kind == 0:
                f, X = field_planes(dx, True)[n]
                ext[step, f, X] = plane
            else:
                rhs[step, DEEP + rim(dx, DEEP, slab)[1] + n] = plane

    def unpack_x(step, part, dx):
        m = (dx + 1) // 2
        for n in range(DEEP):
            if part == 0:
                f, X = field_planes(dx, True)[n]
            else:
                X = DEEP + rim(dx, DEEP, slab)[1] + n
            for c in range(rows // 8):
                piece = slice(ROW + 8 * c, ROW + 8 * c + 8)
                value = x_recv[step, part, m, n, c]
                if part == 0:
                    ext[step, f, X, piece] = value
                else:
                    rhs[step, X, piece] = value

    def unpack_corner(step, part, dx, dy):
        m = (dx + 1) + (dy + 1) // 2
        w = 1 if part == 0 else DEEP - 1
        x, y = rim(dx, w, slab)[1], ROW + rim(dy, w, rows)[1]
        if part == 0:
            for f in range(2):
                ext[step, f, 2 + x, y:y + 1] = c_recv[step, part, m, f:f + 1]
        else:
            for n in range(w):
                rhs[step, DEEP + x + n, y:y + w] = c_recv[step, part, m, w * n:w * n + w]

    def arrive_y(step, part):
        flat = flattened(step, part)
        for dy in (-1, 1):
            messages(step, part, 0, dy).wait_recv()
            for n, base in enumerate(lines(part, dy, True)):
                flat[pl.ds(base, slab, stride=TALL), :] = y_recv[step, part, (dy + 1) // 2, n]

    def arrive_x(step, part):
        for dx in (-1, 1):
            @pl.when(has[-dx])
            def _():
                messages(step, part, dx, 0).wait_recv()
                unpack_x(step, part, dx)
                for dy in (-1, 1):
                    messages(step, part, dx, dy).wait_recv()
                    unpack_corner(step, part, dx, dy)
        for dx in (-1, 1):
            @pl.when(ends[-dx])
            def _():
                for kind in ((0,) if part == 0 else (1, 2)):
                    for k in range(ngy):
                        shear_arrival(step, kind, -dx, k).wait_recv()
                    sheared(step, kind, dx)

    def sent_all(step):
        for part in range(2):
            for dy in (-1, 1):
                messages(step, part, 0, dy).wait_send()
            for dx in (-1, 1):
                @pl.when(has[dx])
                def _():
                    for dy in (0, -1, 1):
                        messages(step, part, dx, dy).wait_send()
        for dx in (-1, 1):
            @pl.when(ends[dx])
            def _():
                for kind in range(3):
                    for k in range(ngy):
                        shear_message(step, kind, dx, k).wait_send()

    half = -0.5 * time_step
    keep = 1.0 - 6.0 * time_step * viscosity
    spread = time_step * viscosity

    def move(c, parts, hu, hv, hw):
        total, ddx, ddy, ddz = parts
        return (keep * c + spread * total) + (hu * ddx + hv * ddy + hw * ddz)

    def mean_flow(x):
        return rate * (x.astype(jnp.float32) + (0.5 - total_x / 2.0))

    lo, hi = ROW, ROW + rows

    def speeds(step, X):
        e = ext.at[step]
        flow = mean_flow(lax.rem(gx * slab + (X - 2) + total_x, total_x))
        u, v, w = e[0, X, lo:hi], e[1, X, lo:hi], e[2, X, lo:hi]
        return u, half * u, half * (v + flow), half * w

    def around(step, f, X):
        e = ext.at[step]
        c = e[f, X, lo:hi]
        return c, stencil(c, e[f, X - 1, lo:hi], e[f, X + 1, lo:hi],
                          e[f, X, lo - 1:hi - 1], e[f, X, lo + 1:hi + 1])

    def provisional(step, planes):
        for i in planes:
            X = i + 2
            u, hu, hv, hw = speeds(step, X)
            for f in range(4):
                c, parts = around(step, f, X)
                value = move(c, parts, hu, hv, hw)
                if f == 1:
                    value = value - (time_step * rate) * u
                if f == 3:
                    value = value - time_step * u
                prov[f, i + 1, lo:hi] = value

    def provisional_x_ghosts(step):
        for X in (1, slab + 2):
            u, hu, hv, hw = speeds(step, X)
            c, parts = around(step, 0, X)
            prov[0, X - 1, lo:hi] = move(c, parts, hu, hv, hw)

    def provisional_y_ghosts(step):
        flat = flattened(step, 0)
        into = prov.reshape(4 * (slab + 2) * TALL, 128)
        place = gx * slab + lax.broadcasted_iota(jnp.int32, (slab, 128), 0)
        flow = mean_flow(place)
        for y in (-1, rows):
            def line(f, x, yy):
                return flat[pl.ds((f * (slab + 4) + 2 + x) * TALL + ROW + yy, slab, stride=TALL), :]

            u, c, w = line(0, 0, y), line(1, 0, y), line(2, 0, y)
            parts = stencil(c, line(1, -1, y), line(1, 1, y), line(1, 0, y - 1), line(1, 0, y + 1))
            value = move(c, parts, half * u, half * (c + flow), half * w) - (time_step * rate) * u
            into[pl.ds((slab + 2 + 1) * TALL + ROW + y, slab, stride=TALL), :] = value

    def divergence(step, planes):
        scale = 0.5 / (6.0 * time_step)
        for i in planes:
            dx = prov[0, i + 2, lo:hi] - prov[0, i, lo:hi]
            dy = prov[1, i + 1, lo + 1:hi + 1] - prov[1, i + 1, lo - 1:hi - 1]
            w = prov[2, i + 1, lo:hi]
            rhs[step, DEEP + i, lo:hi] = scale * (dx + dy + (across(w, -1) - across(w, 1)))

    def relax(step, k, planes):
        r = rhs.at[step]
        top, bottom = ROW - RELAX, ROW + rows + RELAX
        old, new = (press.at[k - 1] if k else r), press.at[k]
        for x in planes:
            X = DEEP + x
            c = old[X, top:bottom]
            total = stencil(c, old[X - 1, top:bottom], old[X + 1, top:bottom],
                            old[X, top - 1:bottom - 1], old[X, top + 1:bottom + 1])[0]
            if k == 0:
                new[X, top:bottom] = -(total * (1.0 / 6.0) + c)
            else:
                new[X, top:bottom] = total * (1.0 / 6.0) - r[X, top:bottom]

    def project(step, planes):
        p = press.at[RELAX - 1]

        def store(f, i, value):
            if step < steps - 1:
                ext[step + 1, f, i + 2, lo:hi] = value
            else:
                out[f, i] = value

        for i in planes:
            X = DEEP + i
            c = p[X, lo:hi]
            store(0, i, prov[0, i + 1, lo:hi] + half * (p[X + 1, lo:hi] - p[X - 1, lo:hi]))
            store(1, i, prov[1, i + 1, lo:hi] + half * (p[X, lo + 1:hi + 1] - p[X, lo - 1:hi - 1]))
            store(2, i, prov[2, i + 1, lo:hi] + half * (across(c, -1) - across(c, 1)))
            store(3, i, prov[3, i + 1, lo:hi])

    fetch.wait()
    inner = jnp.logical_and(gx > 0, gx < ngx - 1)

    @pl.when(inner)
    def _():
        pl.semaphore_wait(barrier, 8)

    @pl.when(jnp.logical_not(inner))
    def _():
        pl.semaphore_wait(barrier, 5 + ngy)

    for step in range(steps):
        if step == 0:
            start_shear(step, 0)
            start_x(step, 0)
            start_y(step, 0)
            fetch_offsets.wait()
        arrive_y(step, 0)
        provisional(step, range(1, slab - 1))
        provisional_y_ghosts(step)
        divergence(step, range(2, slab - 2))
        start_shear(step, 1)
        arrive_x(step, 0)
        provisional(step, (0, slab - 1))
        provisional_x_ghosts(step)
        provisional_y_ghosts(step)
        divergence(step, (0, 1, slab - 2, slab - 1))
        start_shear(step, 2)
        start_x(step, 1)
        start_y(step, 1)
        arrive_y(step, 1)
        for k in range(RELAX):
            relax(step, k, range(k + 1, slab - k - 1))
        early = range(RELAX + 1, slab - RELAX - 1)
        project(step, early)
        sent_all(step)
        arrive_x(step, 1)
        for k in range(RELAX):
            relax(step, k, range(k - RELAX, k + 1))
            relax(step, k, range(slab - k - 1, slab + RELAX - k))
        ends_first = (0, 1, slab - 2, slab - 1)
        project(step, ends_first)
        if step < steps - 1:
            start_shear(step + 1, 0)
            start_x(step + 1, 0)
        project(step, [i for i in range(slab) if i not in ends_first and i not in early])
        if step < steps - 1:
            start_y(step + 1, 0)


def local(ngx, ngy, state, offsets):
    steps = offsets.shape[0]
    fields, slab, rows, depth = state.shape
    f32 = jnp.float32
    return pl.pallas_call(
        functools.partial(kernel, ngx, ngy, steps),
        out_shape=jax.ShapeDtypeStruct(state.shape, f32),
        in_specs=[pl.BlockSpec(memory_space=pl.ANY), pl.BlockSpec(memory_space=pl.ANY)],
        out_specs=pl.BlockSpec(memory_space=pltpu.VMEM),
        scratch_shapes=[
            pltpu.VMEM((steps, fields, slab + 4, TALL, depth), f32),
            pltpu.VMEM((fields, slab + 2, TALL, depth), f32),
            pltpu.VMEM((steps, slab + 2 * DEEP, TALL, depth), f32),
            pltpu.VMEM((RELAX, slab + 2 * DEEP, TALL, depth), f32),
            pltpu.VMEM((steps, 2, 2, DEEP, rows // 8, 8, depth), f32),
            pltpu.VMEM((steps, 2, 2, DEEP, rows // 8, 8, depth), f32),
            pltpu.VMEM((steps, 2, 2, DEEP, slab, depth), f32),
            pltpu.VMEM((steps, 2, 2, DEEP, slab, depth), f32),
            pltpu.VMEM((steps, 2, 4, 16, depth), f32),
            pltpu.VMEM((steps, 2, 4, 16, depth), f32),
            pltpu.SemaphoreType.DMA((steps, 2, 8)),
            pltpu.SemaphoreType.DMA((steps, 2, 8)),
            pltpu.SemaphoreType.DMA((steps, 3, ngy)),
            pltpu.SemaphoreType.DMA((steps, 3, ngy)),
            pltpu.SemaphoreType.DMA((3,)),
            pltpu.SMEM((steps,), jnp.int32),
        ] + [pltpu.VMEM((count, ngy * rows // 8, 8, depth), f32) for count in (DEEP, DEEP - 2, 2)] * steps,
        compiler_params=pltpu.CompilerParams(
            collective_id=0, has_side_effects=True, vmem_limit_bytes=53 * 1024 * 1024 + 256 * 1024
        ),
    )(offsets, state)


def solution(mesh):
    in_specs = (P(None, "gx", "gy", None), P())
    out_specs = P(None, "gx", "gy", None)
    body = functools.partial(local, mesh.shape["gx"], mesh.shape["gy"])
    return jax.shard_map(body, mesh=mesh, in_specs=in_specs, out_specs=out_specs, check_vma=False)
```

```python
import functools

import jax
import jax.numpy as jnp
from jax import lax
from jax.experimental import pallas as pl
from jax.experimental.pallas import tpu as pltpu
from jax.sharding import PartitionSpec as P

RELAX = 4
DEEP = RELAX + 1

time_step = 0.2
viscosity = 0.1

MESH = pl.DeviceIdType.MESH
ROW = 8
TALL = 32


def across(x, shift):
    return pltpu.roll(x, shift % x.shape[-1], x.ndim - 1)


def stencil(c, xm, xp, ym, yp):
    zp, zm = across(c, -1), across(c, 1)
    total = (xp + xm) + (yp + ym) + (zp + zm)
    return total, xp - xm, yp - ym, zp - zm


def kernel(ngx, ngy, steps, offsets_in, state, out, ext, prov, rhs, press,
           x_send, x_recv, y_send, y_recv, c_send, c_recv, send_sem, recv_sem, shear_out, shear_in, local_sem, offsets, *shear_recv):
    slab, rows = state.shape[1], state.shape[2]
    gx, gy = lax.axis_index("gx"), lax.axis_index("gy")
    below, above = lax.rem(gx + ngx - 1, ngx), lax.rem(gx + 1, ngx)
    left, right = lax.rem(gy + ngy - 1, ngy), lax.rem(gy + 1, ngy)
    at_x = {-1: below, 0: gx, 1: above}
    at_y = {-1: left, 0: gy, 1: right}
    has = {-1: gx > 0, 1: gx < ngx - 1}
    ends = {-1: gx == 0, 1: gx == ngx - 1}
    far = {-1: ngx - 1, 1: 0}
    total_x = slab * ngx
    rate = 2.0 / total_x
    own = pl.ds(ROW, rows)

    barrier = pltpu.get_barrier_semaphore()

    def greet(x, y):
        pl.semaphore_signal(barrier, inc=1, device_id=(x, y), device_id_type=MESH)

    for dx in (-1, 1):
        @pl.when(ends[dx])
        def _():
            for k in range(ngy):
                greet(far[dx], k)
    for dx in (-1, 1):
        @pl.when(has[dx])
        def _():
            for dy in (-1, 0, 1):
                greet(at_x[dx], at_y[dy])
    for dy in (-1, 1):
        greet(gx, at_y[dy])

    fetch = pltpu.make_async_copy(state, ext.at[0, :, pl.ds(2, slab), own, :], local_sem.at[0])
    fetch.start()
    fetch_offsets = pltpu.make_async_copy(offsets_in, offsets, local_sem.at[2])
    fetch_offsets.start()

    def remote(src, dst, send, recv, x, y):
        return pltpu.make_async_remote_copy(
            src_ref=src, dst_ref=dst, send_sem=send, recv_sem=recv,
            device_id=(x, y), device_id_type=MESH)

    def rim(side, width, size):
        return (0, size) if side < 0 else (size - width, -width)

    def messages(step, part, dx, dy):
        dev = at_x[dx], at_y[dy]
        if dx == 0:
            n = m = (dy + 1) // 2
            src, dst = y_send.at[step, part, m], y_recv.at[step, part, m]
        elif dy == 0:
            m = (dx + 1) // 2
            n = 2 + m
            src, dst = x_send.at[step, part, m], x_recv.at[step, part, m]
        else:
            m = (dx + 1) + (dy + 1) // 2
            n = 4 + m
            size = pl.ds(0, 8 if part == 0 else 16)
            src, dst = c_send.at[step, part, m, size, :], c_recv.at[step, part, m, size, :]
        return remote(src, dst, send_sem.at[step, part, n], recv_sem.at[step, part, n], *dev)

    def shear_part(kind, dx):
        if kind == 0:
            return 0, DEEP
        deep = DEEP - 2
        if kind == 1:
            return (2 if dx < 0 else 0), deep
        return (0 if dx < 0 else deep), 2

    def shear_slot(step, kind, k):
        return shear_recv[3 * step + kind].at[:, pl.ds(k * (rows // 8), rows // 8), :, :]

    def shear_message(step, kind, dx, k):
        first, count = shear_part(kind, dx)
        src = x_send.at[step, min(kind, 1), (dx + 1) // 2, pl.ds(first, count)]
        return remote(src, shear_slot(step, kind, gy),
                      shear_out.at[step, kind, k], shear_in.at[step, kind, gy], far[dx], k)

    def shear_arrival(step, kind, dx, k):
        slot = shear_slot(step, kind, k)
        return remote(slot, slot, shear_out.at[step, kind, k], shear_in.at[step, kind, k], far[dx], k)

    def field_planes(dx, ghost):
        s2, d2 = rim(dx, 2, slab)
        s1, d1 = rim(dx, 1, slab)
        p2, p1 = (d2, d1) if ghost else (s2, s1)
        return [(0, 2 + p2), (0, 3 + p2), (1, 2 + p1), (2, 2 + p1), (3, 2 + p1)]

    def lines(part, dy, ghost):
        if part == 0:
            s2, d2 = rim(dy, 2, rows)
            s1, d1 = rim(dy, 1, rows)
            p2, p1 = (d2, d1) if ghost else (s2, s1)
            return [(f * (slab + 4) + 2) * TALL + ROW + y
                    for f, y in ((1, p2), (1, p2 + 1), (0, p1), (2, p1), (3, p1))]
        s, d = rim(dy, DEEP, rows)
        return [DEEP * TALL + ROW + (d if ghost else s) + k for k in range(DEEP)]

    def flattened(step, part):
        if part == 0:
            return ext.at[step].reshape(4 * (slab + 4) * TALL, 128)
        return rhs.at[step].reshape((slab + 2 * DEEP) * TALL, 128)

    def pack_x(step, part, dx, first=0, count=DEEP):
        m = (dx + 1) // 2
        for n in range(first, first + count):
            if part == 0:
                f, X = field_planes(dx, False)[n]
            else:
                X = DEEP + rim(dx, DEEP, slab)[0] + n
            for c in range(rows // 8):
                piece = slice(ROW + 8 * c, ROW + 8 * c + 8)
                x_send[step, part, m, n, c] = ext[step, f, X, piece] if part == 0 else rhs[step, X, piece]

    def pack_y(step, part, dy):
        flat = flattened(step, part)
        for n, base in enumerate(lines(part, dy, False)):
            y_send[step, part, (dy + 1) // 2, n] = flat[pl.ds(base, slab, stride=TALL), :]

    def pack_corner(step, part, dx, dy):
        w = 1 if part == 0 else DEEP - 1
        m = (dx + 1) + (dy + 1) // 2
        x, y = rim(dx, w, slab)[0], ROW + rim(dy, w, rows)[0]
        if part == 0:
            for f in range(2):
                c_send[step, part, m, f:f + 1] = ext[step, f, 2 + x, y:y + 1]
        else:
            for n in range(w):
                c_send[step, part, m, w * n:w * n + w] = rhs[step, DEEP + x + n, y:y + w]

    def start_shear(step, kind):
        for dx in (-1, 1):
            @pl.when(ends[dx])
            def _():
                if kind > 0:
                    pack_x(step, 1, dx, *shear_part(kind, dx))
                else:
                    pack_x(step, 0, dx)
                for away in range(ngy):
                    shear_message(step, kind, dx, lax.rem(gy + away, ngy)).start()

    def start_x(step, part):
        for dx in (-1, 1):
            @pl.when(has[dx])
            def _():
                pack_x(step, part, dx)
                messages(step, part, dx, 0).start()
                for dy in (-1, 1):
                    pack_corner(step, part, dx, dy)
                    messages(step, part, dx, dy).start()

    def start_y(step, part):
        for dy in (-1, 1):
            pack_y(step, part, dy)
            messages(step, part, 0, dy).start()

    def sheared(step, kind, dx):
        span = rows * ngy
        shift = span - offsets[step] if dx > 0 else offsets[step]
        start = lax.rem(gy * rows + shift + (span - ROW), span)
        block, within = lax.div(start, 8), lax.rem(start, 8)
        blocks = [lax.rem(block + c, span // 8) for c in range(TALL // 8 + 1)]
        first, count = shear_part(kind, dx)
        for n in range(first, first + count):
            tall = jnp.concatenate([shear_recv[3 * step + kind][n - first, at] for at in blocks], axis=0)
            plane = pltpu.roll(tall, TALL + 8 - within, 0)[:TALL]
            if kind == 0:
                f, X = field_planes(dx, True)[n]
                ext[step, f, X] = plane
            else:
                rhs[step, DEEP + rim(dx, DEEP, slab)[1] + n] = plane

    def unpack_x(step, part, dx):
        m = (dx + 1) // 2
        for n in range(DEEP):
            if part == 0:
                f, X = field_planes(dx, True)[n]
            else:
                X = DEEP + rim(dx, DEEP, slab)[1] + n
            for c in range(rows // 8):
                piece = slice(ROW + 8 * c, ROW + 8 * c + 8)
                value = x_recv[step, part, m, n, c]
                if part == 0:
                    ext[step, f, X, piece] = value
                else:
                    rhs[step, X, piece] = value

    def unpack_corner(step, part, dx, dy):
        m = (dx + 1) + (dy + 1) // 2
        w = 1 if part == 0 else DEEP - 1
        x, y = rim(dx, w, slab)[1], ROW + rim(dy, w, rows)[1]
        if part == 0:
            for f in range(2):
                ext[step, f, 2 + x, y:y + 1] = c_recv[step, part, m, f:f + 1]
        else:
            for n in range(w):
                rhs[step, DEEP + x + n, y:y + w] = c_recv[step, part, m, w * n:w * n + w]

    def arrive_y(step, part):
        flat = flattened(step, part)
        for dy in (-1, 1):
            messages(step, part, 0, dy).wait_recv()
            for n, base in enumerate(lines(part, dy, True)):
                flat[pl.ds(base, slab, stride=TALL), :] = y_recv[step, part, (dy + 1) // 2, n]

    def arrive_x(step, part):
        for dx in (-1, 1):
            @pl.when(has[-dx])
            def _():
                messages(step, part, dx, 0).wait_recv()
                unpack_x(step, part, dx)
                for dy in (-1, 1):
                    messages(step, part, dx, dy).wait_recv()
                    unpack_corner(step, part, dx, dy)
                if part == 1:
                    finish(step, -dx)
        for dx in (-1, 1):
            @pl.when(ends[-dx])
            def _():
                for kind in ((0,) if part == 0 else (1, 2)):
                    for k in range(ngy):
                        shear_arrival(step, kind, -dx, k).wait_recv()
                    sheared(step, kind, dx)
                if part == 1:
                    finish(step, -dx)

    def sent_all(step):
        for part in range(2):
            for dy in (-1, 1):
                messages(step, part, 0, dy).wait_send()
            for dx in (-1, 1):
                @pl.when(has[dx])
                def _():
                    for dy in (0, -1, 1):
                        messages(step, part, dx, dy).wait_send()
        for dx in (-1, 1):
            @pl.when(ends[dx])
            def _():
                for kind in range(3):
                    for k in range(ngy):
                        shear_message(step, kind, dx, k).wait_send()

    half = -0.5 * time_step
    keep = 1.0 - 6.0 * time_step * viscosity
    spread = time_step * viscosity

    def move(c, parts, hu, hv, hw):
        total, ddx, ddy, ddz = parts
        return (keep * c + spread * total) + (hu * ddx + hv * ddy + hw * ddz)

    def mean_flow(x):
        return rate * (x.astype(jnp.float32) + (0.5 - total_x / 2.0))

    lo, hi = ROW, ROW + rows

    def speeds(step, X):
        e = ext.at[step]
        flow = mean_flow(lax.rem(gx * slab + (X - 2) + total_x, total_x))
        u, v, w = e[0, X, lo:hi], e[1, X, lo:hi], e[2, X, lo:hi]
        return u, half * u, half * (v + flow), half * w

    def around(step, f, X):
        e = ext.at[step]
        c = e[f, X, lo:hi]
        return c, stencil(c, e[f, X - 1, lo:hi], e[f, X + 1, lo:hi],
                          e[f, X, lo - 1:hi - 1], e[f, X, lo + 1:hi + 1])

    def provisional(step, planes):
        for i in planes:
            X = i + 2
            u, hu, hv, hw = speeds(step, X)
            for f in range(4):
                c, parts = around(step, f, X)
                value = move(c, parts, hu, hv, hw)
                if f == 1:
                    value = value - (time_step * rate) * u
                if f == 3:
                    value = value - time_step * u
                prov[f, i + 1, lo:hi] = value

    def provisional_x_ghosts(step):
        for X in (1, slab + 2):
            u, hu, hv, hw = speeds(step, X)
            c, parts = around(step, 0, X)
            prov[0, X - 1, lo:hi] = move(c, parts, hu, hv, hw)

    def provisional_y_ghosts(step):
        flat = flattened(step, 0)
        into = prov.reshape(4 * (slab + 2) * TALL, 128)
        place = gx * slab + lax.broadcasted_iota(jnp.int32, (slab, 128), 0)
        flow = mean_flow(place)
        for y in (-1, rows):
            def line(f, x, yy):
                return flat[pl.ds((f * (slab + 4) + 2 + x) * TALL + ROW + yy, slab, stride=TALL), :]

            u, c, w = line(0, 0, y), line(1, 0, y), line(2, 0, y)
            parts = stencil(c, line(1, -1, y), line(1, 1, y), line(1, 0, y - 1), line(1, 0, y + 1))
            value = move(c, parts, half * u, half * (c + flow), half * w) - (time_step * rate) * u
            into[pl.ds((slab + 2 + 1) * TALL + ROW + y, slab, stride=TALL), :] = value

    def divergence(step, planes):
        scale = 0.5 / (6.0 * time_step)
        for i in planes:
            dx = prov[0, i + 2, lo:hi] - prov[0, i, lo:hi]
            dy = prov[1, i + 1, lo + 1:hi + 1] - prov[1, i + 1, lo - 1:hi - 1]
            w = prov[2, i + 1, lo:hi]
            rhs[step, DEEP + i, lo:hi] = scale * (dx + dy + (across(w, -1) - across(w, 1)))

    def relax(step, k, planes):
        r = rhs.at[step]
        top, bottom = ROW - RELAX, ROW + rows + RELAX
        old, new = (press.at[k - 1] if k else r), press.at[k]
        for x in planes:
            X = DEEP + x
            c = old[X, top:bottom]
            total = stencil(c, old[X - 1, top:bottom], old[X + 1, top:bottom],
                            old[X, top - 1:bottom - 1], old[X, top + 1:bottom + 1])[0]
            if k == 0:
                new[X, top:bottom] = -(total * (1.0 / 6.0) + c)
            else:
                new[X, top:bottom] = total * (1.0 / 6.0) - r[X, top:bottom]

    def finish(step, side):
        for k in range(RELAX):
            relax(step, k, range(k - RELAX, k + 1) if side < 0 else range(slab - k - 1, slab + RELAX - k))
        project(step, (0, 1) if side < 0 else (slab - 2, slab - 1))

    def project(step, planes):
        p = press.at[RELAX - 1]

        def store(f, i, value):
            if step < steps - 1:
                ext[step + 1, f, i + 2, lo:hi] = value
            else:
                out[f, i] = value

        for i in planes:
            X = DEEP + i
            c = p[X, lo:hi]
            store(0, i, prov[0, i + 1, lo:hi] + half * (p[X + 1, lo:hi] - p[X - 1, lo:hi]))
            store(1, i, prov[1, i + 1, lo:hi] + half * (p[X, lo + 1:hi + 1] - p[X, lo - 1:hi - 1]))
            store(2, i, prov[2, i + 1, lo:hi] + half * (across(c, -1) - across(c, 1)))
            store(3, i, prov[3, i + 1, lo:hi])

    fetch.wait()
    inner = jnp.logical_and(gx > 0, gx < ngx - 1)

    @pl.when(inner)
    def _():
        pl.semaphore_wait(barrier, 8)

    @pl.when(jnp.logical_not(inner))
    def _():
        pl.semaphore_wait(barrier, 5 + ngy)

    for step in range(steps):
        if step == 0:
            start_shear(step, 0)
            start_x(step, 0)
            start_y(step, 0)
            fetch_offsets.wait()
        arrive_y(step, 0)
        provisional(step, range(1, slab - 1))
        provisional_y_ghosts(step)
        divergence(step, range(2, slab - 2))
        start_shear(step, 1)
        arrive_x(step, 0)
        provisional(step, (0, slab - 1))
        provisional_x_ghosts(step)
        provisional_y_ghosts(step)
        divergence(step, (0, 1, slab - 2, slab - 1))
        start_shear(step, 2)
        start_x(step, 1)
        start_y(step, 1)
        arrive_y(step, 1)
        for k in range(RELAX):
            relax(step, k, range(k + 1, slab - k - 1))
        early = range(RELAX + 1, slab - RELAX - 1)
        project(step, early)
        sent_all(step)
        arrive_x(step, 1)
        if step < steps - 1:
            start_shear(step + 1, 0)
            start_x(step + 1, 0)
        project(step, [i for i in range(2, slab - 2) if i not in early])
        if step < steps - 1:
            start_y(step + 1, 0)


def local(ngx, ngy, state, offsets):
    steps = offsets.shape[0]
    fields, slab, rows, depth = state.shape
    f32 = jnp.float32
    return pl.pallas_call(
        functools.partial(kernel, ngx, ngy, steps),
        out_shape=jax.ShapeDtypeStruct(state.shape, f32),
        in_specs=[pl.BlockSpec(memory_space=pl.ANY), pl.BlockSpec(memory_space=pl.ANY)],
        out_specs=pl.BlockSpec(memory_space=pltpu.VMEM),
        scratch_shapes=[
            pltpu.VMEM((steps, fields, slab + 4, TALL, depth), f32),
            pltpu.VMEM((fields, slab + 2, TALL, depth), f32),
            pltpu.VMEM((steps, slab + 2 * DEEP, TALL, depth), f32),
            pltpu.VMEM((RELAX, slab + 2 * DEEP, TALL, depth), f32),
            pltpu.VMEM((steps, 2, 2, DEEP, rows // 8, 8, depth), f32),
            pltpu.VMEM((steps, 2, 2, DEEP, rows // 8, 8, depth), f32),
            pltpu.VMEM((steps, 2, 2, DEEP, slab, depth), f32),
            pltpu.VMEM((steps, 2, 2, DEEP, slab, depth), f32),
            pltpu.VMEM((steps, 2, 4, 16, depth), f32),
            pltpu.VMEM((steps, 2, 4, 16, depth), f32),
            pltpu.SemaphoreType.DMA((steps, 2, 8)),
            pltpu.SemaphoreType.DMA((steps, 2, 8)),
            pltpu.SemaphoreType.DMA((steps, 3, ngy)),
            pltpu.SemaphoreType.DMA((steps, 3, ngy)),
            pltpu.SemaphoreType.DMA((3,)),
            pltpu.SMEM((steps,), jnp.int32),
        ] + [pltpu.VMEM((count, ngy * rows // 8, 8, depth), f32) for count in (DEEP, DEEP - 2, 2)] * steps,
        compiler_params=pltpu.CompilerParams(
            collective_id=0, has_side_effects=True, vmem_limit_bytes=32 * 1024 * 1024
        ),
    )(pltpu.with_memory_space_constraint(offsets, pltpu.HBM), pltpu.with_memory_space_constraint(state, pltpu.HBM))


def solution(mesh):
    in_specs = (P(None, "gx", "gy", None), P())
    out_specs = P(None, "gx", "gy", None)
    body = functools.partial(local, mesh.shape["gx"], mesh.shape["gy"])
    return jax.shard_map(body, mesh=mesh, in_specs=in_specs, out_specs=out_specs, check_vma=False)
```

```python
import functools

import jax
import jax.numpy as jnp
from jax import lax
from jax.experimental import pallas as pl
from jax.experimental.pallas import tpu as pltpu
from jax.sharding import PartitionSpec as P

RELAX = 4
DEEP = RELAX + 1

time_step = 0.2
viscosity = 0.1

MESH = pl.DeviceIdType.MESH
ROW = 8
TALL = 32


def across(x, shift):
    return pltpu.roll(x, shift % x.shape[-1], x.ndim - 1)


def stencil(c, xm, xp, ym, yp):
    zp, zm = across(c, -1), across(c, 1)
    total = (xp + xm) + (yp + ym) + (zp + zm)
    return total, xp - xm, yp - ym, zp - zm


def kernel(ngx, ngy, steps, offsets_in, state, out, ext, prov, rhs, press,
           x_send, x_recv, y_send, y_recv, c_send, c_recv, send_sem, recv_sem, shear_out, shear_in, local_sem, offsets, *shear_recv):
    slab, rows = state.shape[1], state.shape[2]
    gx, gy = lax.axis_index("gx"), lax.axis_index("gy")
    below, above = lax.rem(gx + ngx - 1, ngx), lax.rem(gx + 1, ngx)
    left, right = lax.rem(gy + ngy - 1, ngy), lax.rem(gy + 1, ngy)
    at_x = {-1: below, 0: gx, 1: above}
    at_y = {-1: left, 0: gy, 1: right}
    has = {-1: gx > 0, 1: gx < ngx - 1}
    ends = {-1: gx == 0, 1: gx == ngx - 1}
    far = {-1: ngx - 1, 1: 0}
    total_x = slab * ngx
    rate = 2.0 / total_x
    own = pl.ds(ROW, rows)

    barrier = pltpu.get_barrier_semaphore()

    def greet(x, y):
        pl.semaphore_signal(barrier, inc=1, device_id=(x, y), device_id_type=MESH)

    for dx in (-1, 1):
        @pl.when(ends[dx])
        def _():
            for k in range(ngy):
                greet(far[dx], k)
    for dx in (-1, 1):
        @pl.when(has[dx])
        def _():
            for dy in (-1, 0, 1):
                greet(at_x[dx], at_y[dy])
    for dy in (-1, 1):
        greet(gx, at_y[dy])

    fetch = pltpu.make_async_copy(state, ext.at[0, :, pl.ds(2, slab), own, :], local_sem.at[0])
    fetch.start()
    fetch_offsets = pltpu.make_async_copy(offsets_in, offsets, local_sem.at[2])
    fetch_offsets.start()

    def remote(src, dst, send, recv, x, y):
        return pltpu.make_async_remote_copy(
            src_ref=src, dst_ref=dst, send_sem=send, recv_sem=recv,
            device_id=(x, y), device_id_type=MESH)

    def rim(side, width, size):
        return (0, size) if side < 0 else (size - width, -width)

    def messages(step, part, dx, dy):
        dev = at_x[dx], at_y[dy]
        if dx == 0:
            n = m = (dy + 1) // 2
            src, dst = y_send.at[step, part, m], y_recv.at[step, part, m]
        elif dy == 0:
            m = (dx + 1) // 2
            n = 2 + m
            src, dst = x_send.at[step, part, m], x_recv.at[step, part, m]
        else:
            m = (dx + 1) + (dy + 1) // 2
            n = 4 + m
            size = pl.ds(0, 8 if part == 0 else 16)
            src, dst = c_send.at[step, part, m, size, :], c_recv.at[step, part, m, size, :]
        return remote(src, dst, send_sem.at[step, part, n], recv_sem.at[step, part, n], *dev)

    def shear_part(kind, dx):
        if kind == 0:
            return 0, DEEP
        deep = DEEP - 2
        if kind == 1:
            return (2 if dx < 0 else 0), deep
        return (0 if dx < 0 else deep), 2

    def shear_slot(step, kind, k):
        return shear_recv[3 * step + kind].at[:, pl.ds(k * (rows // 8), rows // 8), :, :]

    def shear_message(step, kind, dx, k):
        first, count = shear_part(kind, dx)
        src = x_send.at[step, min(kind, 1), (dx + 1) // 2, pl.ds(first, count)]
        return remote(src, shear_slot(step, kind, gy),
                      shear_out.at[step, kind, k], shear_in.at[step, kind, gy], far[dx], k)

    def shear_arrival(step, kind, dx, k):
        slot = shear_slot(step, kind, k)
        return remote(slot, slot, shear_out.at[step, kind, k], shear_in.at[step, kind, k], far[dx], k)

    def field_planes(dx, ghost):
        s2, d2 = rim(dx, 2, slab)
        s1, d1 = rim(dx, 1, slab)
        p2, p1 = (d2, d1) if ghost else (s2, s1)
        return [(0, 2 + p2), (0, 3 + p2), (1, 2 + p1), (2, 2 + p1), (3, 2 + p1)]

    def lines(part, dy, ghost):
        if part == 0:
            s2, d2 = rim(dy, 2, rows)
            s1, d1 = rim(dy, 1, rows)
            p2, p1 = (d2, d1) if ghost else (s2, s1)
            return [(f * (slab + 4) + 2) * TALL + ROW + y
                    for f, y in ((1, p2), (1, p2 + 1), (0, p1), (2, p1), (3, p1))]
        s, d = rim(dy, DEEP, rows)
        return [DEEP * TALL + ROW + (d if ghost else s) + k for k in range(DEEP)]

    def flattened(step, part):
        if part == 0:
            return ext.at[step].reshape(4 * (slab + 4) * TALL, 128)
        return rhs.at[step].reshape((slab + 2 * DEEP) * TALL, 128)

    def pack_x(step, part, dx, first=0, count=DEEP):
        m = (dx + 1) // 2
        for n in range(first, first + count):
            if part == 0:
                f, X = field_planes(dx, False)[n]
            else:
                X = DEEP + rim(dx, DEEP, slab)[0] + n
            for c in range(rows // 8):
                piece = slice(ROW + 8 * c, ROW + 8 * c + 8)
                x_send[step, part, m, n, c] = ext[step, f, X, piece] if part == 0 else rhs[step, X, piece]

    def pack_y(step, part, dy):
        flat = flattened(step, part)
        for n, base in enumerate(lines(part, dy, False)):
            y_send[step, part, (dy + 1) // 2, n] = flat[pl.ds(base, slab, stride=TALL), :]

    def pack_corner(step, part, dx, dy):
        w = 1 if part == 0 else DEEP - 1
        m = (dx + 1) + (dy + 1) // 2
        x, y = rim(dx, w, slab)[0], ROW + rim(dy, w, rows)[0]
        if part == 0:
            for f in range(2):
                c_send[step, part, m, f:f + 1] = ext[step, f, 2 + x, y:y + 1]
        else:
            for n in range(w):
                c_send[step, part, m, w * n:w * n + w] = rhs[step, DEEP + x + n, y:y + w]

    def start_shear(step, kind):
        for dx in (-1, 1):
            @pl.when(ends[dx])
            def _():
                if kind > 0:
                    pack_x(step, 1, dx, *shear_part(kind, dx))
                else:
                    pack_x(step, 0, dx)
                for away in range(ngy):
                    shear_message(step, kind, dx, lax.rem(gy + away, ngy)).start()

    def start_x(step, part):
        for dx in (-1, 1):
            @pl.when(has[dx])
            def _():
                pack_x(step, part, dx)
                messages(step, part, dx, 0).start()
                for dy in (-1, 1):
                    pack_corner(step, part, dx, dy)
                    messages(step, part, dx, dy).start()

    def start_y(step, part):
        for dy in (-1, 1):
            pack_y(step, part, dy)
            messages(step, part, 0, dy).start()

    def sheared(step, kind, dx):
        span = rows * ngy
        shift = span - offsets[step] if dx > 0 else offsets[step]
        start = lax.rem(gy * rows + shift + (span - ROW), span)
        block, within = lax.div(start, 8), lax.rem(start, 8)
        blocks = [lax.rem(block + c, span // 8) for c in range(TALL // 8 + 1)]
        first, count = shear_part(kind, dx)
        for n in range(first, first + count):
            tall = jnp.concatenate([shear_recv[3 * step + kind][n - first, at] for at in blocks], axis=0)
            plane = pltpu.roll(tall, lax.rem(TALL + 8 - within, TALL + 8), 0)[:TALL]
            if kind == 0:
                f, X = field_planes(dx, True)[n]
                ext[step, f, X] = plane
            else:
                rhs[step, DEEP + rim(dx, DEEP, slab)[1] + n] = plane

    def unpack_x(step, part, dx):
        m = (dx + 1) // 2
        for n in range(DEEP):
            if part == 0:
                f, X = field_planes(dx, True)[n]
            else:
                X = DEEP + rim(dx, DEEP, slab)[1] + n
            for c in range(rows // 8):
                piece = slice(ROW + 8 * c, ROW + 8 * c + 8)
                value = x_recv[step, part, m, n, c]
                if part == 0:
                    ext[step, f, X, piece] = value
                else:
                    rhs[step, X, piece] = value

    def unpack_corner(step, part, dx, dy):
        m = (dx + 1) + (dy + 1) // 2
        w = 1 if part == 0 else DEEP - 1
        x, y = rim(dx, w, slab)[1], ROW + rim(dy, w, rows)[1]
        if part == 0:
            for f in range(2):
                ext[step, f, 2 + x, y:y + 1] = c_recv[step, part, m, f:f + 1]
        else:
            for n in range(w):
                rhs[step, DEEP + x + n, y:y + w] = c_recv[step, part, m, w * n:w * n + w]

    def arrive_y(step, part):
        flat = flattened(step, part)
        for dy in (-1, 1):
            messages(step, part, 0, dy).wait_recv()
            for n, base in enumerate(lines(part, dy, True)):
                flat[pl.ds(base, slab, stride=TALL), :] = y_recv[step, part, (dy + 1) // 2, n]

    def arrive_x(step, part):
        for dx in (-1, 1):
            @pl.when(has[-dx])
            def _():
                messages(step, part, dx, 0).wait_recv()
                unpack_x(step, part, dx)
                for dy in (-1, 1):
                    messages(step, part, dx, dy).wait_recv()
                    unpack_corner(step, part, dx, dy)
                if part == 1:
                    finish(step, -dx)
        for dx in (-1, 1):
            @pl.when(ends[-dx])
            def _():
                for kind in ((0,) if part == 0 else (1, 2)):
                    for k in range(ngy):
                        shear_arrival(step, kind, -dx, k).wait_recv()
                    sheared(step, kind, dx)
                if part == 1:
                    finish(step, -dx)

    def sent_all(step):
        for part in range(2):
            for dy in (-1, 1):
                messages(step, part, 0, dy).wait_send()
            for dx in (-1, 1):
                @pl.when(has[dx])
                def _():
                    for dy in (0, -1, 1):
                        messages(step, part, dx, dy).wait_send()
        for dx in (-1, 1):
            @pl.when(ends[dx])
            def _():
                for kind in range(3):
                    for k in range(ngy):
                        shear_message(step, kind, dx, k).wait_send()

    half = -0.5 * time_step
    keep = 1.0 - 6.0 * time_step * viscosity
    spread = time_step * viscosity

    def move(c, parts, hu, hv, hw):
        total, ddx, ddy, ddz = parts
        return (keep * c + spread * total) + (hu * ddx + hv * ddy + hw * ddz)

    def mean_flow(x):
        return rate * (x.astype(jnp.float32) + (0.5 - total_x / 2.0))

    lo, hi = ROW, ROW + rows

    def speeds(step, X):
        e = ext.at[step]
        flow = mean_flow(lax.rem(gx * slab + (X - 2) + total_x, total_x))
        u, v, w = e[0, X, lo:hi], e[1, X, lo:hi], e[2, X, lo:hi]
        return u, half * u, half * (v + flow), half * w

    def around(step, f, X):
        e = ext.at[step]
        c = e[f, X, lo:hi]
        return c, stencil(c, e[f, X - 1, lo:hi], e[f, X + 1, lo:hi],
                          e[f, X, lo - 1:hi - 1], e[f, X, lo + 1:hi + 1])

    def provisional(step, planes):
        for i in planes:
            X = i + 2
            u, hu, hv, hw = speeds(step, X)
            for f in range(4):
                c, parts = around(step, f, X)
                value = move(c, parts, hu, hv, hw)
                if f == 1:
                    value = value - (time_step * rate) * u
                if f == 3:
                    value = value - time_step * u
                prov[f, i + 1, lo:hi] = value

    def provisional_x_ghosts(step):
        for X in (1, slab + 2):
            u, hu, hv, hw = speeds(step, X)
            c, parts = around(step, 0, X)
            prov[0, X - 1, lo:hi] = move(c, parts, hu, hv, hw)

    def provisional_y_ghosts(step):
        flat = flattened(step, 0)
        into = prov.reshape(4 * (slab + 2) * TALL, 128)
        place = gx * slab + lax.broadcasted_iota(jnp.int32, (slab, 128), 0)
        flow = mean_flow(place)
        for y in (-1, rows):
            def line(f, x, yy):
                return flat[pl.ds((f * (slab + 4) + 2 + x) * TALL + ROW + yy, slab, stride=TALL), :]

            u, c, w = line(0, 0, y), line(1, 0, y), line(2, 0, y)
            parts = stencil(c, line(1, -1, y), line(1, 1, y), line(1, 0, y - 1), line(1, 0, y + 1))
            value = move(c, parts, half * u, half * (c + flow), half * w) - (time_step * rate) * u
            into[pl.ds((slab + 2 + 1) * TALL + ROW + y, slab, stride=TALL), :] = value

    def divergence(step, planes):
        scale = 0.5 / (6.0 * time_step)
        for i in planes:
            dx = prov[0, i + 2, lo:hi] - prov[0, i, lo:hi]
            dy = prov[1, i + 1, lo + 1:hi + 1] - prov[1, i + 1, lo - 1:hi - 1]
            w = prov[2, i + 1, lo:hi]
            rhs[step, DEEP + i, lo:hi] = scale * (dx + dy + (across(w, -1) - across(w, 1)))

    def relax(step, k, planes):
        r = rhs.at[step]
        top, bottom = ROW - RELAX, ROW + rows + RELAX
        old, new = (press.at[k - 1] if k else r), press.at[k]
        for x in planes:
            X = DEEP + x
            c = old[X, top:bottom]
            total = stencil(c, old[X - 1, top:bottom], old[X + 1, top:bottom],
                            old[X, top - 1:bottom - 1], old[X, top + 1:bottom + 1])[0]
            if k == 0:
                new[X, top:bottom] = -(total * (1.0 / 6.0) + c)
            else:
                new[X, top:bottom] = total * (1.0 / 6.0) - r[X, top:bottom]

    def finish(step, side):
        for k in range(RELAX):
            relax(step, k, range(k - RELAX, k + 1) if side < 0 else range(slab - k - 1, slab + RELAX - k))
        project(step, (0, 1) if side < 0 else (slab - 2, slab - 1))

    def project(step, planes):
        p = press.at[RELAX - 1]

        def store(f, i, value):
            if step < steps - 1:
                ext[step + 1, f, i + 2, lo:hi] = value
            else:
                out[f, i] = value

        for i in planes:
            X = DEEP + i
            c = p[X, lo:hi]
            store(0, i, prov[0, i + 1, lo:hi] + half * (p[X + 1, lo:hi] - p[X - 1, lo:hi]))
            store(1, i, prov[1, i + 1, lo:hi] + half * (p[X, lo + 1:hi + 1] - p[X, lo - 1:hi - 1]))
            store(2, i, prov[2, i + 1, lo:hi] + half * (across(c, -1) - across(c, 1)))
            store(3, i, prov[3, i + 1, lo:hi])

    fetch.wait()
    inner = jnp.logical_and(gx > 0, gx < ngx - 1)

    @pl.when(inner)
    def _():
        pl.semaphore_wait(barrier, 8)

    @pl.when(jnp.logical_not(inner))
    def _():
        pl.semaphore_wait(barrier, 5 + ngy)

    for step in range(steps):
        if step == 0:
            start_shear(step, 0)
            start_x(step, 0)
            start_y(step, 0)
            fetch_offsets.wait()
        arrive_y(step, 0)
        provisional(step, range(1, slab - 1))
        provisional_y_ghosts(step)
        divergence(step, range(2, slab - 2))
        start_shear(step, 1)
        arrive_x(step, 0)
        provisional(step, (0, slab - 1))
        provisional_x_ghosts(step)
        provisional_y_ghosts(step)
        divergence(step, (0, 1, slab - 2, slab - 1))
        start_shear(step, 2)
        start_x(step, 1)
        start_y(step, 1)
        arrive_y(step, 1)
        for k in range(RELAX):
            relax(step, k, range(k + 1, slab - k - 1))
        early = range(RELAX + 1, slab - RELAX - 1)
        project(step, early)
        sent_all(step)
        arrive_x(step, 1)
        if step < steps - 1:
            start_shear(step + 1, 0)
            start_x(step + 1, 0)
        project(step, [i for i in range(2, slab - 2) if i not in early])
        if step < steps - 1:
            start_y(step + 1, 0)


def local(ngx, ngy, state, offsets):
    steps = offsets.shape[0]
    fields, slab, rows, depth = state.shape
    f32 = jnp.float32
    return pl.pallas_call(
        functools.partial(kernel, ngx, ngy, steps),
        out_shape=jax.ShapeDtypeStruct(state.shape, f32),
        in_specs=[pl.BlockSpec(memory_space=pl.ANY), pl.BlockSpec(memory_space=pl.ANY)],
        out_specs=pl.BlockSpec(memory_space=pltpu.VMEM),
        scratch_shapes=[
            pltpu.VMEM((steps, fields, slab + 4, TALL, depth), f32),
            pltpu.VMEM((fields, slab + 2, TALL, depth), f32),
            pltpu.VMEM((steps, slab + 2 * DEEP, TALL, depth), f32),
            pltpu.VMEM((RELAX, slab + 2 * DEEP, TALL, depth), f32),
            pltpu.VMEM((steps, 2, 2, DEEP, rows // 8, 8, depth), f32),
            pltpu.VMEM((steps, 2, 2, DEEP, rows // 8, 8, depth), f32),
            pltpu.VMEM((steps, 2, 2, DEEP, slab, depth), f32),
            pltpu.VMEM((steps, 2, 2, DEEP, slab, depth), f32),
            pltpu.VMEM((steps, 2, 4, 16, depth), f32),
            pltpu.VMEM((steps, 2, 4, 16, depth), f32),
            pltpu.SemaphoreType.DMA((steps, 2, 8)),
            pltpu.SemaphoreType.DMA((steps, 2, 8)),
            pltpu.SemaphoreType.DMA((steps, 3, ngy)),
            pltpu.SemaphoreType.DMA((steps, 3, ngy)),
            pltpu.SemaphoreType.DMA((3,)),
            pltpu.SMEM((steps,), jnp.int32),
        ] + [pltpu.VMEM((count, ngy * rows // 8, 8, depth), f32) for count in (DEEP, DEEP - 2, 2)] * steps,
        compiler_params=pltpu.CompilerParams(
            collective_id=0, has_side_effects=True, vmem_limit_bytes=32 * 1024 * 1024
        ),
    )(pltpu.with_memory_space_constraint(offsets, pltpu.HBM), pltpu.with_memory_space_constraint(state, pltpu.HBM))


def solution(mesh):
    in_specs = (P(None, "gx", "gy", None), P())
    out_specs = P(None, "gx", "gy", None)
    body = functools.partial(local, mesh.shape["gx"], mesh.shape["gy"])
    return jax.shard_map(body, mesh=mesh, in_specs=in_specs, out_specs=out_specs, check_vma=False)
```
